32 devices in a mesh: pole: 2 (over y), row: 4 (over z), col: 4 (over x, core).
Axes of the slice: x: 2, y: 2, z: 4, core: 2. Of those that a mesh axis runs over, the one named last changes fastest.
Arguments:
- front_h: bfloat16 [1024, 1024], P(('row', 'col')), may hold values from -6 to 6
- front_s: bfloat16 [1024, 1024], P(('row', 'col')), may hold values from -6 to 6
- panel_h: bfloat16 [1024, 256], P('row'), may hold values from -6 to 6
- panel_s: bfloat16 [1024, 256], P('row'), may hold values from -4 to 4
- pivot_h: bfloat16 [256, 256], replicated, may hold values from -1.7 to 8.5, as said below
- pivot_s: bfloat16 [256, 256], replicated, may hold values from -0.1 to 1.5, as said below
- pole_shift: float32 [2, 2], P('pole'), may hold values from -0.5 to 1.5, as said below
- pole_weight: float32 [2, 2], P('pole'), may hold values from -6 to 6
- pattern: int32 [4, 4], replicated, may hold values 0 or 1
- ancestor_inverse: bfloat16 [2, 2, 4, 4, 64, 1024], P('pole', None, None, 'col', None, 'row'), may hold values from -0.1875 to 0.1875
Outputs:
- schur: bfloat16 [2, 2, 4, 4, 64, 1024], P('pole', None, None, 'col', None, 'row')
- density_rows: float32 [1024, 256], P(('row', 'col'), 'pole')
- density_pivot: float32 [256, 256], P(None, 'pole')
The draws below stay inside these ranges and needn't reach their ends.
Inputs may be any that keep to these rules, and one draw needn't show every extreme that they name: `pivot_h`: symmetric; each row's off-diagonal entries sum in magnitude to at most 6.6, the diagonal lies in 8 to 8.5. `pivot_s`: symmetric; each row's off-diagonal entries sum in magnitude to at most 0.33, the diagonal lies in 1 to 1.5. `pole_shift`: column 0 lies in -0.5 to 0.5, column 1 in 0.25 to 1.5.
All inputs are finite; a program needn't handle non-finite values.
Results may differ from the reference program's by a relative error of at most 0.0063.
Values may be sent and summed in bfloat16 or wider, within the bound.
A program may use at most 64 MiB of HBM per device.

```python
import jax
import jax.numpy as jnp
from jax import lax

SUPER = 256
NEWTON = 4
POLES = 2
NB = 4
ORDER = 1024
STRIP = 64
N_ROW = 4
N_COL = 4


def banded_symmetric(key, diag_lo, diag_hi, reach, inner):
    first, second = jax.random.split(key)
    index = jnp.arange(SUPER)
    gap = jnp.abs(index[:, None] - index[None, :])
    sign = jnp.where(jax.random.uniform(first, (SUPER, SUPER)) < 0.5, -1.0, 1.0)
    raw = sign * jax.random.uniform(second, (SUPER, SUPER), jnp.float32, inner * reach, reach)
    upper = index[:, None] < index[None, :]
    symmetric = jnp.where(upper, raw, raw.T)
    band = jnp.where((gap >= 1) & (gap <= 2), symmetric, 0.0)
    diagonal = jax.random.uniform(first, (SUPER,), jnp.float32, diag_lo, diag_hi)
    return band + jnp.diag(diagonal)


def coherent_band(key, diag_lo, diag_hi, lowest, reach):
    first, second, third = jax.random.split(key, 3)
    index = jnp.arange(SUPER)
    gap = jnp.abs(index[:, None] - index[None, :])
    gauge = jnp.where(jax.random.uniform(first, (SUPER,)) < 0.5, -1.0, 1.0)
    raw = jax.random.uniform(second, (SUPER, SUPER), jnp.float32, lowest, reach)
    upper = index[:, None] < index[None, :]
    magnitude = jnp.where(upper, raw, raw.T)
    band = jnp.where((gap >= 1) & (gap <= 2), -gauge[:, None] * gauge[None, :] * magnitude, 0.0)
    diagonal = jax.random.uniform(third, (SUPER,), jnp.float32, diag_lo, diag_hi)
    return band + jnp.diag(diagonal)


def draw_pivot_h(key, part):
    key = jax.random.fold_in(key, 11)
    matrix = coherent_band(key, 8.0, 8.5, 1.4, 1.65)
    return matrix.astype(jnp.bfloat16)


def draw_pivot_s(key, part):
    key = jax.random.fold_in(key, 12)
    matrix = banded_symmetric(key, 1.0, 1.5, 0.08, -1.0)
    return matrix.astype(jnp.bfloat16)


def draw_pole_shift(key, part):
    key = jax.random.fold_in(key, 13)
    first, second = jax.random.split(key)
    real = jax.random.uniform(first, (POLES,), jnp.float32, -0.5, 0.5)
    imag = jax.random.uniform(second, (POLES,), jnp.float32, 0.25, 1.5)
    return jnp.stack([real, imag], axis=1)


def plant(drawn, rng, low, largest):
    dims = drawn.shape
    spot = [jax.random.randint(jax.random.fold_in(rng, axis), (), 0, dims[axis]) for axis in range(len(dims))]
    drawn = drawn.at[tuple(spot)].set(low)
    longest = dims.index(max(dims))
    spot[longest] = (spot[longest] + 1) % dims[longest]
    return drawn.at[tuple(spot)].set(largest)


def levels(stream_key, dims, shards, smallest, top_value):
    factor_of, own = 1.0, jax.random.fold_in(stream_key, 6)
    for axis_at, blocks in shards:
        draws = jnp.exp(jax.random.uniform(jax.random.fold_in(own, axis_at), (blocks,), jnp.float32, smallest / len(shards), top_value / len(shards)))
        factor_of = factor_of * jnp.repeat(draws, dims[axis_at] // blocks).reshape([-1 if axis == axis_at else 1 for axis in range(len(dims))])
    return factor_of


def normal_values(own_key, dims, spread, most, shards=(), kind=jnp.bfloat16):
    gain = levels(own_key, dims, shards, -0.22, 0.18) if shards else 1.0
    array = jax.random.normal(own_key, dims, jnp.float32) * spread * gain
    return jnp.minimum(jnp.maximum(array, -most), most).astype(kind)


def setup_inputs(seed: int = 0) -> dict:
    streams_of = jax.random.split(jax.random.key(seed), 11)
    front_h = normal_values(streams_of[0], (ORDER, ORDER), 1.0, 6.0, ((0, 16),))
    front_s = normal_values(streams_of[1], (ORDER, ORDER), 0.5, 6.0, ((0, 16),))
    panel_h = normal_values(streams_of[2], (ORDER, SUPER), 1.0, 6.0, ((0, 4),))
    panel_s = normal_values(streams_of[3], (ORDER, SUPER), 0.3, 4.0, ((0, 4),))
    pivot_h = draw_pivot_h(jax.random.fold_in(streams_of[10], 71), 0)
    pivot_s = draw_pivot_s(jax.random.fold_in(streams_of[10], 71), 0)
    pole_shift = draw_pole_shift(jax.random.fold_in(streams_of[10], 71), 0)
    pole_weight = normal_values(streams_of[7], (POLES, 2), 2.0, 6.0, ((0, 2),), jnp.float32)
    pattern = plant((jax.random.randint(streams_of[8], (NB, NB), 0, 2) < 1).astype(jnp.int32), jax.random.fold_in(streams_of[8], 1), 0, 1)
    ancestor_inverse = normal_values(streams_of[9], (POLES, 2, N_ROW, N_COL, STRIP, ORDER), ORDER ** -0.5, 0.1875, ((0, 2), (3, 4), (5, 4)))
    return {"front_h": front_h, "front_s": front_s, "panel_h": panel_h, "panel_s": panel_s, "pivot_h": pivot_h, "pivot_s": pivot_s, "pole_shift": pole_shift, "pole_weight": pole_weight, "pattern": pattern, "ancestor_inverse": ancestor_inverse}


highest = lax.Precision.HIGHEST


def complex_matmul(left_real, left_imag, right_real, right_imag):
    real = jnp.dot(left_real, right_real, precision=highest, preferred_element_type=jnp.float32) - jnp.dot(left_imag, right_imag, precision=highest, preferred_element_type=jnp.float32)
    imag = jnp.dot(left_real, right_imag, precision=highest, preferred_element_type=jnp.float32) + jnp.dot(left_imag, right_real, precision=highest, preferred_element_type=jnp.float32)
    return real, imag


def complex_einsum(form, left_real, left_imag, right_real, right_imag):
    real = jnp.einsum(form, left_real, right_real, precision=highest) - jnp.einsum(form, left_imag, right_imag, precision=highest)
    imag = jnp.einsum(form, left_real, right_imag, precision=highest) + jnp.einsum(form, left_imag, right_real, precision=highest)
    return real, imag


def invert_pivot(pivot_h, pivot_s, shift_real, shift_imag, sweeps):
    matrix_real = pivot_h.astype(jnp.float32) - shift_real * pivot_s.astype(jnp.float32)
    matrix_imag = -shift_imag * pivot_s.astype(jnp.float32)
    diag_real = jnp.diagonal(matrix_real)
    diag_imag = jnp.diagonal(matrix_imag)
    denom = diag_real * diag_real + diag_imag * diag_imag
    identity = jnp.eye(matrix_real.shape[0], dtype=jnp.float32)

    def advance(index, state):
        approx_real, approx_imag = state
        prod_real, prod_imag = complex_matmul(matrix_real, matrix_imag, approx_real, approx_imag)
        return complex_matmul(approx_real, approx_imag, 2.0 * identity - prod_real, -prod_imag)

    start = (jnp.diag(diag_real / denom), jnp.diag(-diag_imag / denom))
    return lax.fori_loop(0, sweeps, advance, start)


def reference(front_h, front_s, panel_h, panel_s, pivot_h, pivot_s, pole_shift, pole_weight, pattern, ancestor_inverse):
    block_mask = jnp.repeat(jnp.repeat(pattern.astype(jnp.float32), SUPER, axis=0), SUPER, axis=1)
    hamil = front_h.astype(jnp.float32)
    margin = front_s.astype(jnp.float32)
    panel_hf = panel_h.astype(jnp.float32)
    panel_sf = panel_s.astype(jnp.float32)
    density_rows = jnp.zeros((ORDER, SUPER), jnp.float32)
    density_pivot = jnp.zeros((SUPER, SUPER), jnp.float32)
    schur_list = []
    for pole in range(POLES):
        shift_real = pole_shift[pole, 0]
        shift_imag = pole_shift[pole, 1]
        weight_real = pole_weight[pole, 0]
        weight_imag = pole_weight[pole, 1]
        inv_real, inv_imag = invert_pivot(pivot_h, pivot_s, shift_real, shift_imag, NEWTON)
        coupling_real = (panel_hf - shift_real * panel_sf).astype(jnp.bfloat16).astype(jnp.float32)
        coupling_imag = (-shift_imag * panel_sf).astype(jnp.bfloat16).astype(jnp.float32)
        solved_real, solved_imag = complex_matmul(coupling_real, coupling_imag, inv_real, inv_imag)
        solved_real = solved_real.astype(jnp.bfloat16).astype(jnp.float32)
        solved_imag = solved_imag.astype(jnp.bfloat16).astype(jnp.float32)
        front_real = block_mask * (hamil - shift_real * margin)
        front_imag = block_mask * (-shift_imag * margin)
        update_real, update_imag = complex_einsum("gk,ik->gi", solved_real, solved_imag, coupling_real, coupling_imag)
        schur = jnp.stack([front_real - update_real, front_imag - update_imag]).astype(jnp.bfloat16)
        schur_list.append(schur.reshape(2, N_ROW, N_COL, STRIP, ORDER))
        ancestor = ancestor_inverse[pole].astype(jnp.float32).reshape(2, ORDER, ORDER)
        part_real, part_imag = complex_einsum("gi,gk->ik", ancestor[0], ancestor[1], solved_real, solved_imag)
        column_real = -part_real
        column_imag = -part_imag
        corr_real, corr_imag = complex_einsum("sk,sl->kl", solved_real, solved_imag, column_real, column_imag)
        block_real = inv_real - corr_real
        block_imag = inv_imag - corr_imag
        density_rows = density_rows + (weight_real * column_imag + weight_imag * column_real)
        density_pivot = density_pivot + (weight_real * block_imag + weight_imag * block_real)
    return jnp.stack(schur_list), density_rows, density_pivot
```

```python
import functools

import jax
import jax.numpy as jnp
from jax import lax
from jax.experimental import pallas as pl
from jax.experimental.pallas import tpu as pltpu
from jax.sharding import PartitionSpec as P

MESH = pl.DeviceIdType.MESH
F32 = jnp.float32
BF16 = jnp.bfloat16


def nn(left, right):
    return lax.dot_general(left, right, (((1,), (0,)), ((), ())), preferred_element_type=F32)


def nt(left, right):
    return lax.dot_general(left, right, (((1,), (1,)), ((), ())), preferred_element_type=F32)


def complex_product(dot, left, right):
    left_real, left_imag = left
    right_real, right_imag = right
    real = dot(left_real, right_real) - dot(left_imag, right_imag)
    imag = dot(left_real, right_imag) + dot(left_imag, right_real)
    return real, imag


def rounded(pair):
    return pair[0].astype(BF16), pair[1].astype(BF16)


def split(pair):
    high = rounded(pair)
    low = rounded((pair[0] - high[0].astype(F32), pair[1] - high[1].astype(F32)))
    return high, low


def plus(left, right):
    return left[0] + right[0], left[1] + right[1]


def couple(rows_h, rows_s, shift_real, shift_imag):
    margin = rows_s.astype(F32)
    real = rows_h.astype(F32) - shift_real * margin
    return real.astype(BF16), (-shift_imag * margin).astype(BF16)


def pivot_inverse(pivot_h, pivot_s, shift_real, shift_imag):
    size = pivot_h.shape[0]
    margin = pivot_s.astype(F32)
    real = pivot_h.astype(F32) - shift_real * margin
    imag = -shift_imag * margin
    on_diagonal = lax.broadcasted_iota(jnp.int32, (size, size), 0) == lax.broadcasted_iota(
        jnp.int32, (size, size), 1
    )
    only_real = jnp.where(on_diagonal, real, 0.0)
    only_imag = jnp.where(on_diagonal, imag, 0.0)

    def start(axis):
        diag_real = jnp.sum(only_real, axis=axis, keepdims=True)
        diag_imag = jnp.sum(only_imag, axis=axis, keepdims=True)
        denom = diag_real * diag_real + diag_imag * diag_imag
        return diag_real / denom, -diag_imag / denom

    left_real, left_imag = start(1)
    right_real, right_imag = start(0)
    identity = jnp.where(on_diagonal, 1.0, 0.0)
    first = (
        identity - (left_real * real - left_imag * imag),
        -(left_real * imag + left_imag * real),
    )
    first_b = rounded(first)
    second = complex_product(nn, first_b, first_b)
    second_b = rounded(second)
    third = complex_product(nn, second_b, first_b)
    fourth_b = rounded(complex_product(nn, second_b, second_b))
    total = plus(plus((identity + first[0], first[1]), second), third)
    total = plus(total, complex_product(nn, rounded(total), fourth_b))
    eighth_b = rounded(complex_product(nn, fourth_b, fourth_b))
    total = plus(total, complex_product(nn, rounded(total), eighth_b))
    return (
        total[0] * right_real - total[1] * right_imag,
        total[0] * right_imag + total[1] * right_real,
    )


def step(
    rows,
    cols,
    poles,
    shift,
    weight,
    pattern,
    front_h,
    front_s,
    panel_h,
    panel_s,
    pivot_h,
    pivot_s,
    ancestor,
    schur_out,
    rows_out,
    pivot_out,
    piv_v,
    own_panel,
    far_panel,
    far_front,
    anc_v,
    schur_v,
    part_rows,
    part_piv,
    send_rows,
    send_piv,
    recv_rows,
    recv_piv,
    layer_send,
    layer_recv,
    final_piv,
    final_rows,
    local_sem,
    panel_ssem,
    panel_rsem,
    front_ssem,
    front_rsem,
    rows_ssem,
    rows_rsem,
    piv_ssem,
    piv_rsem,
    layer_ssem,
    layer_rsem,
    last_ssem,
    last_rsem,
    out_sem,
):
    row = lax.axis_index("row")
    col = lax.axis_index("col")
    pole = lax.axis_index("pole")
    layer = poles * cols
    me = pole * cols + col
    width = front_h.shape[0]
    block = panel_h.shape[0]
    size = pivot_h.shape[0]
    piece = size // poles
    strip = size // cols

    def row_peer(offset):
        return lax.rem(row + offset, rows)

    def layer_peer(offset):
        index = lax.rem(me + offset, layer)
        return index, {"pole": index // cols, "col": lax.rem(index, cols)}

    barrier = pltpu.get_barrier_semaphore()
    for offset in range(1, rows):
        pl.semaphore_signal(
            barrier, inc=1, device_id={"row": row_peer(offset)}, device_id_type=MESH
        )
    for offset in range(1, layer):
        pl.semaphore_signal(
            barrier, inc=1, device_id=layer_peer(offset)[1], device_id_type=MESH
        )

    here = pl.ds(pl.multiple_of(col * width, width), width)
    mine = pl.ds(pl.multiple_of(row * block, block), block)
    local = [
        pltpu.make_async_copy(source, target, local_sem.at[index])
        for index, (source, target) in enumerate(
            [
                (pivot_h, piv_v.at[0]),
                (pivot_s, piv_v.at[1]),
                (panel_h, own_panel.at[0]),
                (panel_s, own_panel.at[1]),
                (ancestor, anc_v),
                (panel_h.at[here, :], far_panel.at[0, row]),
                (panel_s.at[here, :], far_panel.at[1, row]),
                (front_h.at[:, mine], far_front.at[0, row]),
                (front_s.at[:, mine], far_front.at[1, row]),
            ]
        )
    ]
    for copy in local:
        copy.start()
    pl.semaphore_wait(barrier, rows - 1 + layer - 1)

    panel_sends = []
    panel_recvs = []
    front_sends = []
    front_recvs = []
    for offset in range(1, rows):
        to = row_peer(offset)
        origin = lax.rem(row + rows - offset, rows)
        for part, source in enumerate((panel_h, panel_s)):
            panel_sends.append(
                pltpu.make_async_remote_copy(
                    src_ref=source.at[here, :],
                    dst_ref=far_panel.at[part, row],
                    send_sem=panel_ssem.at[part, offset - 1],
                    recv_sem=panel_rsem.at[part, offset - 1],
                    device_id={"row": to},
                    device_id_type=MESH,
                )
            )
            panel_recvs.append(
                pltpu.make_async_remote_copy(
                    src_ref=source.at[here, :],
                    dst_ref=far_panel.at[part, origin],
                    send_sem=panel_ssem.at[part, offset - 1],
                    recv_sem=panel_rsem.at[part, offset - 1],
                    device_id={"row": to},
                    device_id_type=MESH,
                )
            )
        theirs = pl.ds(pl.multiple_of(to * block, block), block)
        for part, source in enumerate((front_h, front_s)):
            front_sends.append(
                pltpu.make_async_remote_copy(
                    src_ref=source.at[:, theirs],
                    dst_ref=far_front.at[part, row],
                    send_sem=front_ssem.at[part, offset - 1],
                    recv_sem=front_rsem.at[part, offset - 1],
                    device_id={"row": to},
                    device_id_type=MESH,
                )
            )
            front_recvs.append(
                pltpu.make_async_remote_copy(
                    src_ref=source.at[:, theirs],
                    dst_ref=far_front.at[part, origin],
                    send_sem=front_ssem.at[part, offset - 1],
                    recv_sem=front_rsem.at[part, offset - 1],
                    device_id={"row": to},
                    device_id_type=MESH,
                )
            )
    for copy in panel_sends + front_sends:
        copy.start()

    shift_real = shift[0, 0]
    shift_imag = shift[0, 1]
    weight_real = weight[0, 0]
    weight_imag = weight[0, 1]

    local[0].wait()
    local[1].wait()
    inverse = pivot_inverse(piv_v[0], piv_v[1], shift_real, shift_imag)
    inv_high, inv_low = split(inverse)
    for copy in local[2:]:
        copy.wait()
    coupling = couple(own_panel[0], own_panel[1], shift_real, shift_imag)
    flipped = rounded(
        plus(
            complex_product(nt, inv_high, coupling),
            complex_product(nt, inv_low, coupling),
        )
    )
    anc = (
        anc_v[0].reshape(rows * width, block).T,
        anc_v[1].reshape(rows * width, block).T,
    )

    for copy in panel_recvs:
        copy.wait_recv()
    far_coupling = couple(
        far_panel[0].reshape(rows * width, size),
        far_panel[1].reshape(rows * width, size),
        shift_real,
        shift_imag,
    )
    solved = rounded(
        plus(
            complex_product(nn, far_coupling, inv_high),
            complex_product(nn, far_coupling, inv_low),
        )
    )
    part = complex_product(nn, anc, solved)
    weighted_imag = -(weight_real * part[1] + weight_imag * part[0])
    weighted_real = -(weight_real * part[0] - weight_imag * part[1])

    def scatter(value, kept, sent, height):
        for index in range(layer):
            tile = value[
                (index % cols) * height : (index % cols + 1) * height,
                (index // cols) * piece : (index // cols + 1) * piece,
            ]
            kept[index] = tile
            sent[index] = tile.astype(BF16)

    def exchange(sent, received, ssem, rsem):
        copies = []
        for offset in range(1, layer):
            index, device = layer_peer(offset)
            copies.append(
                pltpu.make_async_remote_copy(
                    src_ref=sent.at[index],
                    dst_ref=received.at[offset - 1],
                    send_sem=ssem.at[offset - 1],
                    recv_sem=rsem.at[offset - 1],
                    device_id=device,
                    device_id_type=MESH,
                )
            )
        for copy in copies:
            copy.start()
        return copies

    corr = nn(flipped[0], weighted_imag.astype(BF16)) + nn(
        flipped[1], weighted_real.astype(BF16)
    )
    share = (weight_real * inverse[1] + weight_imag * inverse[0]) * (1.0 / (rows * cols)) - corr
    scatter(share, part_piv, send_piv, strip)
    piv_copies = exchange(send_piv, recv_piv, piv_ssem, piv_rsem)
    scatter(weighted_imag, part_rows, send_rows, width)
    rows_copies = exchange(send_rows, recv_rows, rows_ssem, rows_rsem)

    update = complex_product(nt, solved, coupling)

    for copy in piv_copies:
        copy.wait_recv()
    layer_sum = part_piv[me]
    for offset in range(layer - 1):
        layer_sum = layer_sum + recv_piv[offset].astype(F32)
    layer_send[...] = layer_sum
    layer_copies = [
        pltpu.make_async_remote_copy(
            src_ref=layer_send,
            dst_ref=layer_recv.at[offset - 1],
            send_sem=layer_ssem.at[offset - 1],
            recv_sem=layer_rsem.at[offset - 1],
            device_id={"row": row_peer(offset)},
            device_id_type=MESH,
        )
        for offset in range(1, rows)
    ]
    for copy in layer_copies:
        copy.start()

    for copy in front_recvs:
        copy.wait_recv()
    for index in range(rows):
        flag = pattern[index, row].astype(F32)
        margin = far_front[1, index].astype(F32)
        hamil = far_front[0, index].astype(F32)
        at = slice(index * width, (index + 1) * width)
        schur_v[0, index] = (flag * (hamil - shift_real * margin) - update[0][at]).astype(BF16)
        schur_v[1, index] = (flag * (-shift_imag * margin) - update[1][at]).astype(BF16)
    schur_copy = pltpu.make_async_copy(schur_v, schur_out, out_sem.at[0])
    schur_copy.start()

    for copy in layer_copies:
        copy.wait_recv()
    whole = layer_sum
    for offset in range(rows - 1):
        whole = whole + layer_recv[offset]
    final_piv[col] = whole
    last_copies = []
    last_recvs = []
    for offset in range(1, cols):
        to = lax.rem(col + offset, cols)
        origin = lax.rem(col + cols - offset, cols)
        for slot, group in ((col, last_copies), (origin, last_recvs)):
            group.append(
                pltpu.make_async_remote_copy(
                    src_ref=final_piv.at[col],
                    dst_ref=final_piv.at[slot],
                    send_sem=last_ssem.at[offset - 1],
                    recv_sem=last_rsem.at[offset - 1],
                    device_id={"col": to},
                    device_id_type=MESH,
                )
            )
    for copy in last_copies:
        copy.start()

    for copy in rows_copies:
        copy.wait_recv()
    rows_sum = part_rows[me]
    for offset in range(layer - 1):
        rows_sum = rows_sum + recv_rows[offset].astype(F32)
    final_rows[...] = rows_sum
    rows_copy = pltpu.make_async_copy(final_rows, rows_out, out_sem.at[1])
    rows_copy.start()

    for copy in last_recvs:
        copy.wait_recv()
    pivot_copy = pltpu.make_async_copy(final_piv, pivot_out, out_sem.at[2])
    pivot_copy.start()
    for copy in panel_sends + front_sends + piv_copies + rows_copies:
        copy.wait_send()
    for copy in layer_copies + last_copies:
        copy.wait_send()
    schur_copy.wait()
    rows_copy.wait()
    pivot_copy.wait()


def shards(
    rows,
    cols,
    poles,
    front_h,
    front_s,
    panel_h,
    panel_s,
    pivot_h,
    pivot_s,
    pole_shift,
    pole_weight,
    pattern,
    ancestor_inverse,
):
    width = front_h.shape[0]
    block = panel_h.shape[0]
    size = pivot_h.shape[0]
    piece = size // poles
    strip = size // cols
    layer = poles * cols
    ancestor = ancestor_inverse.reshape(2, rows, width, block)
    smem = pl.BlockSpec(memory_space=pltpu.SMEM)
    anywhere = pl.BlockSpec(memory_space=pl.ANY)
    dma = pltpu.SemaphoreType.DMA
    schur, rows_out, pivot_out = pl.pallas_call(
        functools.partial(step, rows, cols, poles),
        out_shape=(
            jax.ShapeDtypeStruct((2, rows, width, block), BF16),
            jax.ShapeDtypeStruct((width, piece), F32),
            jax.ShapeDtypeStruct((cols, strip, piece), F32),
        ),
        in_specs=[smem] * 3 + [anywhere] * 7,
        out_specs=(anywhere,) * 3,
        scratch_shapes=[
            pltpu.VMEM((2, size, size), BF16),
            pltpu.VMEM((2, block, size), BF16),
            pltpu.VMEM((2, rows, width, size), BF16),
            pltpu.VMEM((2, rows, width, block), BF16),
            pltpu.VMEM((2, rows, width, block), BF16),
            pltpu.VMEM((2, rows, width, block), BF16),
            pltpu.VMEM((layer, width, piece), F32),
            pltpu.VMEM((layer, strip, piece), F32),
            pltpu.VMEM((layer, width, piece), BF16),
            pltpu.VMEM((layer, strip, piece), BF16),
            pltpu.VMEM((layer - 1, width, piece), BF16),
            pltpu.VMEM((layer - 1, strip, piece), BF16),
            pltpu.VMEM((strip, piece), F32),
            pltpu.VMEM((rows - 1, strip, piece), F32),
            pltpu.VMEM((cols, strip, piece), F32),
            pltpu.VMEM((width, piece), F32),
            dma((9,)),
            dma((2, rows - 1)),
            dma((2, rows - 1)),
            dma((2, rows - 1)),
            dma((2, rows - 1)),
            dma((layer - 1,)),
            dma((layer - 1,)),
            dma((layer - 1,)),
            dma((layer - 1,)),
            dma((rows - 1,)),
            dma((rows - 1,)),
            dma((cols - 1,)),
            dma((cols - 1,)),
            dma((3,)),
        ],
        compiler_params=pltpu.CompilerParams(
            collective_id=0, has_side_effects=True, vmem_limit_bytes=48 * 1024 * 1024
        ),
        name="front_step",
    )(
        pole_shift,
        pole_weight,
        pattern,
        front_h,
        front_s,
        panel_h,
        panel_s,
        pivot_h,
        pivot_s,
        ancestor,
    )
    return (
        schur.reshape(ancestor_inverse.shape),
        rows_out,
        pivot_out.reshape(size, piece),
    )


def solution(mesh):
    sizes = dict(mesh.shape)
    in_specs = (
        P(("row", "col"), None),
        P(("row", "col"), None),
        P("row", None),
        P("row", None),
        P(),
        P(),
        P("pole", None),
        P("pole", None),
        P(),
        P("pole", None, None, "col", None, "row"),
    )
    out_specs = (
        P("pole", None, None, "col", None, "row"),
        P(("row", "col"), "pole"),
        P(None, "pole"),
    )
    body = functools.partial(shards, sizes["row"], sizes["col"], sizes["pole"])
    return jax.shard_map(body, mesh=mesh, in_specs=in_specs, out_specs=out_specs, check_vma=False)
```

```python
import functools

import jax
import jax.numpy as jnp
from jax import lax
from jax.experimental import pallas as pl
from jax.experimental.pallas import tpu as pltpu
from jax.sharding import PartitionSpec as P

MESH = pl.DeviceIdType.MESH
F32 = jnp.float32
BF16 = jnp.bfloat16


def nn(left, right):
    return lax.dot_general(left, right, (((1,), (0,)), ((), ())), preferred_element_type=F32)


def nt(left, right):
    return lax.dot_general(left, right, (((1,), (1,)), ((), ())), preferred_element_type=F32)


def side(pair):
    return jnp.concatenate(pair, axis=1)


def below(pair):
    real, imag = pair
    return jnp.concatenate([side((real, imag)), side((-imag, real))], axis=0)


def across(pair):
    real, imag = pair
    return jnp.concatenate([side((real, -imag)), side((imag, real))], axis=0)


def halves(value):
    middle = value.shape[1] // 2
    return value[:, :middle], value[:, middle:]


def product(left, right):
    return halves(nn(side(left), below(right)))


def product_nt(left, right):
    return halves(nt(side(left), across(right)))


def rounded(pair):
    return pair[0].astype(BF16), pair[1].astype(BF16)


def split(pair):
    high = rounded(pair)
    low = rounded((pair[0] - high[0].astype(F32), pair[1] - high[1].astype(F32)))
    return high, low


def plus(left, right):
    return left[0] + right[0], left[1] + right[1]


def couple(rows_h, rows_s, shift_real, shift_imag):
    margin = rows_s.astype(F32)
    real = rows_h.astype(F32) - shift_real * margin
    return real.astype(BF16), (-shift_imag * margin).astype(BF16)


def pivot_inverse(pivot_h, pivot_s, shift_real, shift_imag):
    size = pivot_h.shape[0]
    margin = pivot_s.astype(F32)
    real = pivot_h.astype(F32) - shift_real * margin
    imag = -shift_imag * margin
    on_diagonal = lax.broadcasted_iota(jnp.int32, (size, size), 0) == lax.broadcasted_iota(
        jnp.int32, (size, size), 1
    )
    only_real = jnp.where(on_diagonal, real, 0.0)
    only_imag = jnp.where(on_diagonal, imag, 0.0)

    def start(axis):
        diag_real = jnp.sum(only_real, axis=axis, keepdims=True)
        diag_imag = jnp.sum(only_imag, axis=axis, keepdims=True)
        denom = diag_real * diag_real + diag_imag * diag_imag
        return diag_real / denom, -diag_imag / denom

    left_real, left_imag = start(1)
    right_real, right_imag = start(0)
    identity = jnp.where(on_diagonal, 1.0, 0.0)
    first = (
        identity - (left_real * real - left_imag * imag),
        -(left_real * imag + left_imag * real),
    )
    first_b = rounded(first)
    first_below = below(first_b)
    second = halves(nn(side(first_b), first_below))
    second_b = rounded(second)
    wide = nn(side(second_b), jnp.concatenate([first_below, below(second_b)], axis=1))
    third = halves(wide[:, : 2 * size])
    fourth_b = rounded(halves(wide[:, 2 * size :]))
    total = plus(plus((identity + first[0], first[1]), second), third)
    tall = nn(
        jnp.concatenate([side(fourth_b), side(rounded(total))], axis=0), below(fourth_b)
    )
    eighth_b = rounded(halves(tall[:size]))
    total = plus(total, halves(tall[size:]))
    total = plus(total, product(rounded(total), eighth_b))
    return (
        total[0] * right_real - total[1] * right_imag,
        total[0] * right_imag + total[1] * right_real,
    )


def step(
    rows,
    cols,
    poles,
    shift_hbm,
    weight_hbm,
    pattern_hbm,
    front_h,
    front_s,
    panel_h,
    panel_s,
    pivot_h,
    pivot_s,
    ancestor,
    schur_out,
    rows_out,
    pivot_out,
    shift,
    weight,
    pattern,
    piv_v,
    own_panel,
    far_panel,
    far_front,
    anc_v,
    schur_v,
    final_rows,
    final_piv,
    part_rows,
    part_piv,
    send_rows,
    send_piv,
    recv_rows,
    recv_piv,
    layer_send,
    layer_recv,
    local_sem,
    panel_ssem,
    panel_rsem,
    front_ssem,
    front_rsem,
    rows_ssem,
    rows_rsem,
    piv_ssem,
    piv_rsem,
    layer_ssem,
    layer_rsem,
    last_ssem,
    last_rsem,
    out_sem,
):
    row = lax.axis_index("row")
    col = lax.axis_index("col")
    pole = lax.axis_index("pole")
    layer = poles * cols
    me = pole * cols + col
    width = front_h.shape[0]
    block = panel_h.shape[0]
    size = pivot_h.shape[0]
    piece = size // poles
    strip = size // cols

    def row_peer(offset):
        return lax.rem(row + offset, rows)

    def layer_peer(offset):
        index = lax.rem(me + offset, layer)
        return index, {"pole": index // cols, "col": lax.rem(index, cols)}

    barrier = pltpu.get_barrier_semaphore()
    for offset in range(1, rows):
        pl.semaphore_signal(
            barrier, inc=1, device_id={"row": row_peer(offset)}, device_id_type=MESH
        )
    for offset in range(1, layer):
        pl.semaphore_signal(
            barrier, inc=1, device_id=layer_peer(offset)[1], device_id_type=MESH
        )

    here = pl.ds(pl.multiple_of(col * width, width), width)
    mine = pl.ds(pl.multiple_of(row * block, block), block)
    local = [
        pltpu.make_async_copy(source, target, local_sem.at[index])
        for index, (source, target) in enumerate(
            [
                (shift_hbm, shift),
                (pivot_h, piv_v.at[0]),
                (pivot_s, piv_v.at[1]),
                (weight_hbm, weight),
                (pattern_hbm, pattern),
                (panel_h, own_panel.at[0]),
                (panel_s, own_panel.at[1]),
                (ancestor, anc_v),
                (panel_h.at[here, :], far_panel.at[0, row]),
                (panel_s.at[here, :], far_panel.at[1, row]),
                (front_h.at[:, mine], far_front.at[0, row]),
                (front_s.at[:, mine], far_front.at[1, row]),
            ]
        )
    ]
    for copy in local:
        copy.start()
    pl.semaphore_wait(barrier, rows - 1 + layer - 1)

    panel_sends = []
    panel_recvs = []
    front_sends = []
    front_recvs = []
    for offset in range(1, rows):
        to = row_peer(offset)
        origin = lax.rem(row + rows - offset, rows)
        for part, source in enumerate((panel_h, panel_s)):
            panel_sends.append(
                pltpu.make_async_remote_copy(
                    src_ref=source.at[here, :],
                    dst_ref=far_panel.at[part, row],
                    send_sem=panel_ssem.at[part, offset - 1],
                    recv_sem=panel_rsem.at[part, offset - 1],
                    device_id={"row": to},
                    device_id_type=MESH,
                )
            )
            panel_recvs.append(
                pltpu.make_async_remote_copy(
                    src_ref=source.at[here, :],
                    dst_ref=far_panel.at[part, origin],
                    send_sem=panel_ssem.at[part, offset - 1],
                    recv_sem=panel_rsem.at[part, offset - 1],
                    device_id={"row": to},
                    device_id_type=MESH,
                )
            )
        theirs = pl.ds(pl.multiple_of(to * block, block), block)
        for part, source in enumerate((front_h, front_s)):
            front_sends.append(
                pltpu.make_async_remote_copy(
                    src_ref=source.at[:, theirs],
                    dst_ref=far_front.at[part, row],
                    send_sem=front_ssem.at[part, offset - 1],
                    recv_sem=front_rsem.at[part, offset - 1],
                    device_id={"row": to},
                    device_id_type=MESH,
                )
            )
            front_recvs.append(
                pltpu.make_async_remote_copy(
                    src_ref=source.at[:, theirs],
                    dst_ref=far_front.at[part, origin],
                    send_sem=front_ssem.at[part, offset - 1],
                    recv_sem=front_rsem.at[part, offset - 1],
                    device_id={"row": to},
                    device_id_type=MESH,
                )
            )
    for copy in panel_sends:
        copy.start()

    for copy in local[:3]:
        copy.wait()
    shift_real = shift[0, 0]
    shift_imag = shift[0, 1]
    inverse = pivot_inverse(piv_v[0], piv_v[1], shift_real, shift_imag)
    inv_high, inv_low = split(inverse)
    for copy in local[3:]:
        copy.wait()
    weight_real = weight[0, 0]
    weight_imag = weight[0, 1]
    coupling = couple(own_panel[0], own_panel[1], shift_real, shift_imag)
    coupling_across = across(coupling)
    flipped = rounded(
        halves(nt(side(inv_high), coupling_across) + nt(side(inv_low), coupling_across))
    )
    anc = (
        anc_v[0].reshape(rows * width, block),
        anc_v[1].reshape(rows * width, block),
    )
    swept = product_nt(flipped, anc)
    swept_both = side(
        rounded(
            (
                weight_real * swept[1] + weight_imag * swept[0],
                weight_real * swept[0] - weight_imag * swept[1],
            )
        )
    )
    own_share = (weight_real * inverse[1] + weight_imag * inverse[0]) * (1.0 / (rows * cols))
    anc_flipped = side((anc[0].T, anc[1].T))
    inv_below = jnp.concatenate([below(inv_high), below(inv_low)], axis=0)

    for copy in panel_sends:
        copy.wait_send()
    for copy in front_sends:
        copy.start()
    for copy in panel_recvs:
        copy.wait_recv()
    far_coupling = side(
        couple(
            far_panel[0].reshape(rows * width, size),
            far_panel[1].reshape(rows * width, size),
            shift_real,
            shift_imag,
        )
    )
    solved = rounded(halves(nn(jnp.concatenate([far_coupling, far_coupling], axis=1), inv_below)))

    def scatter(value, kept, sent, height):
        for index in range(layer):
            tile = value[
                (index % cols) * height : (index % cols + 1) * height,
                (index // cols) * piece : (index // cols + 1) * piece,
            ]
            kept[index] = tile
            sent[index] = tile.astype(BF16)

    def exchange(sent, received, ssem, rsem):
        copies = []
        for offset in range(1, layer):
            index, device = layer_peer(offset)
            copies.append(
                pltpu.make_async_remote_copy(
                    src_ref=sent.at[index],
                    dst_ref=received.at[offset - 1],
                    send_sem=ssem.at[offset - 1],
                    recv_sem=rsem.at[offset - 1],
                    device_id=device,
                    device_id_type=MESH,
                )
            )
        for copy in copies:
            copy.start()
        return copies

    share = own_share + nn(swept_both, jnp.concatenate(solved, axis=0))
    scatter(share, part_piv, send_piv, strip)
    piv_copies = exchange(send_piv, recv_piv, piv_ssem, piv_rsem)
    part = halves(nn(anc_flipped, below(solved)))
    weighted_imag = -(weight_real * part[1] + weight_imag * part[0])
    scatter(weighted_imag, part_rows, send_rows, width)
    rows_copies = exchange(send_rows, recv_rows, rows_ssem, rows_rsem)

    update = halves(nt(side(solved), coupling_across))

    for copy in piv_copies:
        copy.wait_recv()
    layer_sum = part_piv[me]
    for offset in range(layer - 1):
        layer_sum = layer_sum + recv_piv[offset].astype(F32)
    layer_send[...] = layer_sum.astype(BF16)
    layer_copies = [
        pltpu.make_async_remote_copy(
            src_ref=layer_send,
            dst_ref=layer_recv.at[offset - 1],
            send_sem=layer_ssem.at[offset - 1],
            recv_sem=layer_rsem.at[offset - 1],
            device_id={"row": row_peer(offset)},
            device_id_type=MESH,
        )
        for offset in range(1, rows)
    ]
    for copy in layer_copies:
        copy.start()

    for copy in front_recvs:
        copy.wait_recv()
    for index in range(rows):
        flag = pattern[index, row].astype(F32)
        margin = far_front[1, index].astype(F32)
        hamil = far_front[0, index].astype(F32)
        at = slice(index * width, (index + 1) * width)
        schur_v[0, index] = (flag * (hamil - shift_real * margin) - update[0][at]).astype(BF16)
        schur_v[1, index] = (flag * (-shift_imag * margin) - update[1][at]).astype(BF16)

    schur_copy = pltpu.make_async_copy(schur_v, schur_out, out_sem.at[0])
    schur_copy.start()

    for copy in layer_copies:
        copy.wait_recv()
    whole = layer_sum
    for offset in range(rows - 1):
        whole = whole + layer_recv[offset].astype(F32)
    final_piv[...] = whole
    own_copy = pltpu.make_async_copy(final_piv, pivot_out.at[col], out_sem.at[2])
    own_copy.start()
    last_copies = []
    last_recvs = []
    for offset in range(1, cols):
        to = lax.rem(col + offset, cols)
        origin = lax.rem(col + cols - offset, cols)
        for slot, group in ((col, last_copies), (origin, last_recvs)):
            group.append(
                pltpu.make_async_remote_copy(
                    src_ref=final_piv,
                    dst_ref=pivot_out.at[slot],
                    send_sem=last_ssem.at[offset - 1],
                    recv_sem=last_rsem.at[offset - 1],
                    device_id={"col": to},
                    device_id_type=MESH,
                )
            )
    for copy in last_copies:
        copy.start()

    for copy in rows_copies:
        copy.wait_recv()
    rows_sum = part_rows[me]
    for offset in range(layer - 1):
        rows_sum = rows_sum + recv_rows[offset].astype(F32)
    final_rows[...] = rows_sum
    rows_copy = pltpu.make_async_copy(final_rows, rows_out, out_sem.at[1])
    rows_copy.start()

    for copy in last_recvs:
        copy.wait_recv()
    for copy in front_sends + piv_copies + rows_copies:
        copy.wait_send()
    for copy in layer_copies + last_copies:
        copy.wait_send()
    schur_copy.wait()
    rows_copy.wait()
    own_copy.wait()


def hand_over(*refs):
    sources, targets, sem = refs[:3], refs[3:6], refs[6]
    copies = [
        pltpu.make_async_copy(source, target, sem.at[index])
        for index, (source, target) in enumerate(zip(sources, targets))
    ]
    for copy in copies:
        copy.start()
    for copy in copies:
        copy.wait()


def shards(
    rows,
    cols,
    poles,
    front_h,
    front_s,
    panel_h,
    panel_s,
    pivot_h,
    pivot_s,
    pole_shift,
    pole_weight,
    pattern,
    ancestor_inverse,
):
    width = front_h.shape[0]
    block = panel_h.shape[0]
    size = pivot_h.shape[0]
    piece = size // poles
    strip = size // cols
    layer = poles * cols
    ancestor = ancestor_inverse.reshape(2, rows, width, block)
    hbm = pl.BlockSpec(memory_space=pl.ANY)
    dma = pltpu.SemaphoreType.DMA
    out_shape = (
        jax.ShapeDtypeStruct((2, rows, width, block), BF16),
        jax.ShapeDtypeStruct((width, piece), F32),
        jax.ShapeDtypeStruct((cols, strip, piece), F32),
    )
    found = pl.pallas_call(
        functools.partial(step, rows, cols, poles),
        out_shape=out_shape,
        in_specs=[hbm] * 10,
        out_specs=(hbm,) * 3,
        scratch_shapes=[
            pltpu.SMEM(pole_shift.shape, F32),
            pltpu.SMEM(pole_weight.shape, F32),
            pltpu.SMEM(pattern.shape, jnp.int32),
            pltpu.VMEM((2, size, size), BF16),
            pltpu.VMEM((2, block, size), BF16),
            pltpu.VMEM((2, rows, width, size), BF16),
            pltpu.VMEM((2, rows, width, block), BF16),
            pltpu.VMEM((2, rows, width, block), BF16),
            pltpu.VMEM((2, rows, width, block), BF16),
            pltpu.VMEM((width, piece), F32),
            pltpu.VMEM((strip, piece), F32),
            pltpu.VMEM((layer, width, piece), F32),
            pltpu.VMEM((layer, strip, piece), F32),
            pltpu.VMEM((layer, width, piece), BF16),
            pltpu.VMEM((layer, strip, piece), BF16),
            pltpu.VMEM((layer - 1, width, piece), BF16),
            pltpu.VMEM((layer - 1, strip, piece), BF16),
            pltpu.VMEM((strip, piece), BF16),
            pltpu.VMEM((rows - 1, strip, piece), BF16),
            dma((12,)),
            dma((2, rows - 1)),
            dma((2, rows - 1)),
            dma((2, rows - 1)),
            dma((2, rows - 1)),
            dma((layer - 1,)),
            dma((layer - 1,)),
            dma((layer - 1,)),
            dma((layer - 1,)),
            dma((rows - 1,)),
            dma((rows - 1,)),
            dma((cols - 1,)),
            dma((cols - 1,)),
            dma((3,)),
        ],
        compiler_params=pltpu.CompilerParams(
            collective_id=0, has_side_effects=True, vmem_limit_bytes=60 * 1024 * 1024
        ),
        name="front_step",
    )(
        pole_shift,
        pole_weight,
        pattern,
        front_h,
        front_s,
        panel_h,
        panel_s,
        pivot_h,
        pivot_s,
        ancestor,
    )
    schur, rows_out, pivot_out = pl.pallas_call(
        hand_over,
        out_shape=out_shape,
        in_specs=[hbm] * 3,
        out_specs=(hbm,) * 3,
        scratch_shapes=[dma((3,))],
        compiler_params=pltpu.CompilerParams(vmem_limit_bytes=60 * 1024 * 1024),
        name="hand_over",
    )(*found)
    return (
        schur.reshape(ancestor_inverse.shape),
        rows_out,
        pivot_out.reshape(size, piece),
    )


def solution(mesh):
    sizes = dict(mesh.shape)
    in_specs = (
        P(("row", "col"), None),
        P(("row", "col"), None),
        P("row", None),
        P("row", None),
        P(),
        P(),
        P("pole", None),
        P("pole", None),
        P(),
        P("pole", None, None, "col", None, "row"),
    )
    out_specs = (
        P("pole", None, None, "col", None, "row"),
        P(("row", "col"), "pole"),
        P(None, "pole"),
    )
    body = functools.partial(shards, sizes["row"], sizes["col"], sizes["pole"])
    return jax.shard_map(body, mesh=mesh, in_specs=in_specs, out_specs=out_specs, check_vma=False)
```

```python
import functools

import jax
import jax.numpy as jnp
from jax import lax
from jax.experimental import pallas as pl
from jax.experimental.pallas import tpu as pltpu
from jax.sharding import PartitionSpec as P

MESH = pl.DeviceIdType.MESH
F32 = jnp.float32
BF16 = jnp.bfloat16


def nn(left, right):
    return lax.dot_general(left, right, (((1,), (0,)), ((), ())), preferred_element_type=F32)


def nt(left, right):
    return lax.dot_general(left, right, (((1,), (1,)), ((), ())), preferred_element_type=F32)


def side(pair):
    return jnp.concatenate(pair, axis=1)


def below(pair):
    real, imag = pair
    return jnp.concatenate([side((real, imag)), side((-imag, real))], axis=0)


def across(pair):
    real, imag = pair
    return jnp.concatenate([side((real, -imag)), side((imag, real))], axis=0)


def halves(value):
    middle = value.shape[1] // 2
    return value[:, :middle], value[:, middle:]


def product(left, right):
    return halves(nn(side(left), below(right)))


def product_nt(left, right):
    return halves(nt(side(left), across(right)))


def rounded(pair):
    return pair[0].astype(BF16), pair[1].astype(BF16)


def split(pair):
    high = rounded(pair)
    low = rounded((pair[0] - high[0].astype(F32), pair[1] - high[1].astype(F32)))
    return high, low


def plus(left, right):
    return left[0] + right[0], left[1] + right[1]


def couple(rows_h, rows_s, shift_real, shift_imag):
    margin = rows_s.astype(F32)
    real = rows_h.astype(F32) - shift_real * margin
    return real.astype(BF16), (-shift_imag * margin).astype(BF16)


def pivot_inverse(pivot_h, pivot_s, shift_real, shift_imag):
    size = pivot_h.shape[0]
    margin = pivot_s.astype(F32)
    real = pivot_h.astype(F32) - shift_real * margin
    imag = -shift_imag * margin
    on_diagonal = lax.broadcasted_iota(jnp.int32, (size, size), 0) == lax.broadcasted_iota(
        jnp.int32, (size, size), 1
    )
    only_real = jnp.where(on_diagonal, real, 0.0)
    only_imag = jnp.where(on_diagonal, imag, 0.0)

    def start(axis):
        diag_real = jnp.sum(only_real, axis=axis, keepdims=True)
        diag_imag = jnp.sum(only_imag, axis=axis, keepdims=True)
        denom = diag_real * diag_real + diag_imag * diag_imag
        return diag_real / denom, -diag_imag / denom

    left_real, left_imag = start(1)
    right_real, right_imag = start(0)
    identity = jnp.where(on_diagonal, 1.0, 0.0)
    first = (
        identity - (left_real * real - left_imag * imag),
        -(left_real * imag + left_imag * real),
    )
    first_b = rounded(first)
    first_below = below(first_b)
    second = halves(nn(side(first_b), first_below))
    second_b = rounded(second)
    wide = nn(side(second_b), jnp.concatenate([first_below, below(second_b)], axis=1))
    third = halves(wide[:, : 2 * size])
    fourth_b = rounded(halves(wide[:, 2 * size :]))
    total = plus(plus((identity + first[0], first[1]), second), third)
    tall = nn(
        jnp.concatenate([side(fourth_b), side(rounded(total))], axis=0), below(fourth_b)
    )
    eighth_b = rounded(halves(tall[:size]))
    total = plus(total, halves(tall[size:]))
    total = plus(total, product(rounded(total), eighth_b))
    return (
        total[0] * right_real - total[1] * right_imag,
        total[0] * right_imag + total[1] * right_real,
    )


def step(
    rows,
    cols,
    poles,
    shift_hbm,
    weight_hbm,
    pattern_hbm,
    front_h,
    front_s,
    panel_h,
    panel_s,
    pivot_h,
    pivot_s,
    ancestor,
    schur_out,
    rows_out,
    pivot_out,
    shift,
    weight,
    pattern,
    piv_v,
    own_panel,
    far_panel,
    far_front,
    anc_v,
    schur_v,
    final_rows,
    final_piv,
    part_rows,
    part_piv,
    send_rows,
    send_piv,
    recv_rows,
    recv_piv,
    layer_send,
    layer_recv,
    pass_ssem,
    pass_rsem,
    local_sem,
    panel_ssem,
    panel_rsem,
    front_ssem,
    front_rsem,
    rows_ssem,
    rows_rsem,
    piv_ssem,
    piv_rsem,
    layer_ssem,
    layer_rsem,
    last_ssem,
    last_rsem,
    out_sem,
):
    row = lax.axis_index("row")
    col = lax.axis_index("col")
    pole = lax.axis_index("pole")
    layer = poles * cols
    me = pole * cols + col
    width = front_h.shape[0]
    block = panel_h.shape[0]
    size = pivot_h.shape[0]
    piece = size // poles
    strip = size // cols

    def row_peer(offset):
        return lax.rem(row + offset, rows)

    def layer_peer(offset):
        index = lax.rem(me + offset, layer)
        return index, {"pole": index // cols, "col": lax.rem(index, cols)}

    barrier = pltpu.get_barrier_semaphore()
    for offset in range(1, rows):
        pl.semaphore_signal(
            barrier, inc=1, device_id={"row": row_peer(offset)}, device_id_type=MESH
        )
    for offset in range(1, layer):
        pl.semaphore_signal(
            barrier, inc=1, device_id=layer_peer(offset)[1], device_id_type=MESH
        )

    here = pl.ds(pl.multiple_of(col * width, width), width)
    mine = pl.ds(pl.multiple_of(row * block, block), block)
    local = [
        pltpu.make_async_copy(source, target, local_sem.at[index])
        for index, (source, target) in enumerate(
            [
                (shift_hbm, shift),
                (pivot_h, piv_v.at[0]),
                (pivot_s, piv_v.at[1]),
                (weight_hbm, weight),
                (pattern_hbm, pattern),
                (panel_h, own_panel.at[0]),
                (panel_s, own_panel.at[1]),
                (ancestor, anc_v),
                (panel_h.at[here, :], far_panel.at[0, row]),
                (panel_s.at[here, :], far_panel.at[1, row]),
                (front_h.at[:, mine], far_front.at[0, row]),
                (front_s.at[:, mine], far_front.at[1, row]),
            ]
        )
    ]
    for copy in local:
        copy.start()
    pl.semaphore_wait(barrier, rows - 1 + layer - 1)

    shares = poles if width % (16 * poles) == 0 else 1
    height = width // shares
    first = pl.multiple_of(pole * height if shares > 1 else 0, height)
    held = pl.ds(first, height)
    source_rows = pl.ds(pl.multiple_of(col * width + first, height), height)
    panel_sends = []
    panel_recvs = []
    panel_passes = []
    passed_recvs = []
    front_sends = []
    front_recvs = []
    for offset in range(1, rows):
        to = row_peer(offset)
        origin = lax.rem(row + rows - offset, rows)
        for part, source in enumerate((panel_h, panel_s)):
            panel_sends.append(
                pltpu.make_async_remote_copy(
                    src_ref=source.at[source_rows, :],
                    dst_ref=far_panel.at[part, row, held],
                    send_sem=panel_ssem.at[part, offset - 1],
                    recv_sem=panel_rsem.at[part, offset - 1],
                    device_id={"row": to},
                    device_id_type=MESH,
                )
            )
            panel_recvs.append(
                pltpu.make_async_remote_copy(
                    src_ref=source.at[source_rows, :],
                    dst_ref=far_panel.at[part, origin, held],
                    send_sem=panel_ssem.at[part, offset - 1],
                    recv_sem=panel_rsem.at[part, offset - 1],
                    device_id={"row": to},
                    device_id_type=MESH,
                )
            )
            for hop in range(1, shares):
                giver = lax.rem(pole + shares - hop, shares)
                theirs = pl.ds(pl.multiple_of(giver * height, height), height)
                for rows_of, group in ((held, panel_passes), (theirs, passed_recvs)):
                    group.append(
                        pltpu.make_async_remote_copy(
                            src_ref=far_panel.at[part, origin, held],
                            dst_ref=far_panel.at[part, origin, rows_of],
                            send_sem=pass_ssem.at[part, offset - 1, hop - 1],
                            recv_sem=pass_rsem.at[part, offset - 1, hop - 1],
                            device_id={"pole": lax.rem(pole + hop, shares)},
                            device_id_type=MESH,
                        )
                    )
        theirs = pl.ds(pl.multiple_of(to * block, block), block)
        for part, source in enumerate((front_h, front_s)):
            front_sends.append(
                pltpu.make_async_remote_copy(
                    src_ref=source.at[:, theirs],
                    dst_ref=far_front.at[part, row],
                    send_sem=front_ssem.at[part, offset - 1],
                    recv_sem=front_rsem.at[part, offset - 1],
                    device_id={"row": to},
                    device_id_type=MESH,
                )
            )
            front_recvs.append(
                pltpu.make_async_remote_copy(
                    src_ref=source.at[:, theirs],
                    dst_ref=far_front.at[part, origin],
                    send_sem=front_ssem.at[part, offset - 1],
                    recv_sem=front_rsem.at[part, offset - 1],
                    device_id={"row": to},
                    device_id_type=MESH,
                )
            )
    for copy in panel_sends:
        copy.start()

    for copy in local[:3]:
        copy.wait()
    shift_real = shift[0, 0]
    shift_imag = shift[0, 1]
    inverse = pivot_inverse(piv_v[0], piv_v[1], shift_real, shift_imag)
    inv_high, inv_low = split(inverse)
    for copy in panel_recvs:
        copy.wait_recv()
    for copy in panel_passes:
        copy.start()
    for copy in panel_sends:
        copy.wait_send()
    for copy in front_sends:
        copy.start()
    for copy in local[3:]:
        copy.wait()
    weight_real = weight[0, 0]
    weight_imag = weight[0, 1]
    coupling = couple(own_panel[0], own_panel[1], shift_real, shift_imag)
    coupling_across = across(coupling)
    flipped = rounded(
        halves(nt(side(inv_high), coupling_across) + nt(side(inv_low), coupling_across))
    )
    anc = (
        anc_v[0].reshape(rows * width, block),
        anc_v[1].reshape(rows * width, block),
    )
    swept = product_nt(flipped, anc)
    swept_both = side(
        rounded(
            (
                weight_real * swept[1] + weight_imag * swept[0],
                weight_real * swept[0] - weight_imag * swept[1],
            )
        )
    )
    own_share = (weight_real * inverse[1] + weight_imag * inverse[0]) * (1.0 / (rows * cols))
    anc_flipped = side((anc[0].T, anc[1].T))
    inv_below = jnp.concatenate([below(inv_high), below(inv_low)], axis=0)

    for copy in passed_recvs:
        copy.wait_recv()
    far_coupling = side(
        couple(
            far_panel[0].reshape(rows * width, size),
            far_panel[1].reshape(rows * width, size),
            shift_real,
            shift_imag,
        )
    )
    solved = rounded(halves(nn(jnp.concatenate([far_coupling, far_coupling], axis=1), inv_below)))

    def scatter(value, kept, sent, height):
        for index in range(layer):
            tile = value[
                (index % cols) * height : (index % cols + 1) * height,
                (index // cols) * piece : (index // cols + 1) * piece,
            ]
            kept[index] = tile
            sent[index] = tile.astype(BF16)

    def exchange(sent, received, ssem, rsem):
        copies = []
        for offset in range(1, layer):
            index, device = layer_peer(offset)
            copies.append(
                pltpu.make_async_remote_copy(
                    src_ref=sent.at[index],
                    dst_ref=received.at[offset - 1],
                    send_sem=ssem.at[offset - 1],
                    recv_sem=rsem.at[offset - 1],
                    device_id=device,
                    device_id_type=MESH,
                )
            )
        for copy in copies:
            copy.start()
        return copies

    share = own_share + nn(swept_both, jnp.concatenate(solved, axis=0))
    scatter(share, part_piv, send_piv, strip)
    piv_copies = exchange(send_piv, recv_piv, piv_ssem, piv_rsem)
    part = halves(nn(anc_flipped, below(solved)))
    weighted_imag = -(weight_real * part[1] + weight_imag * part[0])
    scatter(weighted_imag, part_rows, send_rows, width)
    rows_copies = exchange(send_rows, recv_rows, rows_ssem, rows_rsem)

    update = halves(nt(side(solved), coupling_across))

    for copy in piv_copies:
        copy.wait_recv()
    layer_sum = part_piv[me]
    for offset in range(layer - 1):
        layer_sum = layer_sum + recv_piv[offset].astype(F32)
    layer_send[...] = layer_sum.astype(BF16)
    layer_copies = [
        pltpu.make_async_remote_copy(
            src_ref=layer_send,
            dst_ref=layer_recv.at[offset - 1],
            send_sem=layer_ssem.at[offset - 1],
            recv_sem=layer_rsem.at[offset - 1],
            device_id={"row": row_peer(offset)},
            device_id_type=MESH,
        )
        for offset in range(1, rows)
    ]
    for copy in layer_copies:
        copy.start()

    for copy in layer_copies:
        copy.wait_recv()
    whole = layer_sum
    for offset in range(rows - 1):
        whole = whole + layer_recv[offset].astype(F32)
    final_piv[...] = whole
    own_copy = pltpu.make_async_copy(final_piv, pivot_out.at[col], out_sem.at[2])
    own_copy.start()
    last_copies = []
    last_recvs = []
    for offset in range(1, cols):
        to = lax.rem(col + offset, cols)
        origin = lax.rem(col + cols - offset, cols)
        for slot, group in ((col, last_copies), (origin, last_recvs)):
            group.append(
                pltpu.make_async_remote_copy(
                    src_ref=final_piv,
                    dst_ref=pivot_out.at[slot],
                    send_sem=last_ssem.at[offset - 1],
                    recv_sem=last_rsem.at[offset - 1],
                    device_id={"col": to},
                    device_id_type=MESH,
                )
            )
    for copy in last_copies:
        copy.start()

    for copy in front_recvs:
        copy.wait_recv()
    for index in range(rows):
        flag = pattern[index, row].astype(F32)
        margin = far_front[1, index].astype(F32)
        hamil = far_front[0, index].astype(F32)
        at = slice(index * width, (index + 1) * width)
        schur_v[0, index] = (flag * (hamil - shift_real * margin) - update[0][at]).astype(BF16)
        schur_v[1, index] = (flag * (-shift_imag * margin) - update[1][at]).astype(BF16)

    schur_copy = pltpu.make_async_copy(schur_v, schur_out, out_sem.at[0])
    schur_copy.start()

    for copy in rows_copies:
        copy.wait_recv()
    rows_sum = part_rows[me]
    for offset in range(layer - 1):
        rows_sum = rows_sum + recv_rows[offset].astype(F32)
    final_rows[...] = rows_sum
    rows_copy = pltpu.make_async_copy(final_rows, rows_out, out_sem.at[1])
    rows_copy.start()

    for copy in last_recvs:
        copy.wait_recv()
    for copy in panel_passes + front_sends + piv_copies + rows_copies:
        copy.wait_send()
    for copy in layer_copies + last_copies:
        copy.wait_send()
    schur_copy.wait()
    rows_copy.wait()
    own_copy.wait()


def shards(
    rows,
    cols,
    poles,
    front_h,
    front_s,
    panel_h,
    panel_s,
    pivot_h,
    pivot_s,
    pole_shift,
    pole_weight,
    pattern,
    ancestor_inverse,
):
    width = front_h.shape[0]
    block = panel_h.shape[0]
    size = pivot_h.shape[0]
    piece = size // poles
    strip = size // cols
    layer = poles * cols
    ancestor = ancestor_inverse.reshape(2, rows, width, block)
    hbm = pl.BlockSpec(memory_space=pl.ANY)
    dma = pltpu.SemaphoreType.DMA
    out_shape = (
        jax.ShapeDtypeStruct((2, rows, width, block), BF16),
        jax.ShapeDtypeStruct((width, piece), F32),
        jax.ShapeDtypeStruct((cols, strip, piece), F32),
    )
    found = pl.pallas_call(
        functools.partial(step, rows, cols, poles),
        out_shape=out_shape,
        in_specs=[hbm] * 10,
        out_specs=(hbm,) * 3,
        scratch_shapes=[
            pltpu.SMEM(pole_shift.shape, F32),
            pltpu.SMEM(pole_weight.shape, F32),
            pltpu.SMEM(pattern.shape, jnp.int32),
            pltpu.VMEM((2, size, size), BF16),
            pltpu.VMEM((2, block, size), BF16),
            pltpu.VMEM((2, rows, width, size), BF16),
            pltpu.VMEM((2, rows, width, block), BF16),
            pltpu.VMEM((2, rows, width, block), BF16),
            pltpu.VMEM((2, rows, width, block), BF16),
            pltpu.VMEM((width, piece), F32),
            pltpu.VMEM((strip, piece), F32),
            pltpu.VMEM((layer, width, piece), F32),
            pltpu.VMEM((layer, strip, piece), F32),
            pltpu.VMEM((layer, width, piece), BF16),
            pltpu.VMEM((layer, strip, piece), BF16),
            pltpu.VMEM((layer - 1, width, piece), BF16),
            pltpu.VMEM((layer - 1, strip, piece), BF16),
            pltpu.VMEM((strip, piece), BF16),
            pltpu.VMEM((rows - 1, strip, piece), BF16),
            dma((2, rows - 1, poles - 1)),
            dma((2, rows - 1, poles - 1)),
            dma((12,)),
            dma((2, rows - 1)),
            dma((2, rows - 1)),
            dma((2, rows - 1)),
            dma((2, rows - 1)),
            dma((layer - 1,)),
            dma((layer - 1,)),
            dma((layer - 1,)),
            dma((layer - 1,)),
            dma((rows - 1,)),
            dma((rows - 1,)),
            dma((cols - 1,)),
            dma((cols - 1,)),
            dma((3,)),
        ],
        compiler_params=pltpu.CompilerParams(
            collective_id=0, has_side_effects=True, vmem_limit_bytes=60 * 1024 * 1024
        ),
        name="front_step",
    )(
        pole_shift,
        pole_weight,
        pattern,
        front_h,
        front_s,
        panel_h,
        panel_s,
        pivot_h,
        pivot_s,
        ancestor,
    )
    schur, rows_out, pivot_out = found
    return (
        schur.reshape(ancestor_inverse.shape),
        rows_out,
        pivot_out.reshape(size, piece),
    )


def solution(mesh):
    sizes = dict(mesh.shape)
    in_specs = (
        P(("row", "col"), None),
        P(("row", "col"), None),
        P("row", None),
        P("row", None),
        P(),
        P(),
        P("pole", None),
        P("pole", None),
        P(),
        P("pole", None, None, "col", None, "row"),
    )
    out_specs = (
        P("pole", None, None, "col", None, "row"),
        P(("row", "col"), "pole"),
        P(None, "pole"),
    )
    body = functools.partial(shards, sizes["row"], sizes["col"], sizes["pole"])
    return jax.shard_map(body, mesh=mesh, in_specs=in_specs, out_specs=out_specs, check_vma=False)
```

```python
import functools

import jax
import jax.numpy as jnp
from jax import lax
from jax.experimental import pallas as pl
from jax.experimental.pallas import tpu as pltpu
from jax.sharding import PartitionSpec as P

MESH = pl.DeviceIdType.MESH
F32 = jnp.float32
BF16 = jnp.bfloat16


def nn(left, right):
    return lax.dot_general(left, right, (((1,), (0,)), ((), ())), preferred_element_type=F32)


def nt(left, right):
    return lax.dot_general(left, right, (((1,), (1,)), ((), ())), preferred_element_type=F32)


def side(pair):
    return jnp.concatenate(pair, axis=1)


def below(pair):
    real, imag = pair
    return jnp.concatenate([side((real, imag)), side((-imag, real))], axis=0)


def across(pair):
    real, imag = pair
    return jnp.concatenate([side((real, -imag)), side((imag, real))], axis=0)


def halves(value):
    middle = value.shape[1] // 2
    return value[:, :middle], value[:, middle:]


def product(left, right):
    return halves(nn(side(left), below(right)))


def product_nt(left, right):
    return halves(nt(side(left), across(right)))


def rounded(pair):
    return pair[0].astype(BF16), pair[1].astype(BF16)


def split(pair):
    high = rounded(pair)
    low = rounded((pair[0] - high[0].astype(F32), pair[1] - high[1].astype(F32)))
    return high, low


def plus(left, right):
    return left[0] + right[0], left[1] + right[1]


def couple(rows_h, rows_s, shift_real, shift_imag):
    margin = rows_s.astype(F32)
    real = rows_h.astype(F32) - shift_real * margin
    return real.astype(BF16), (-shift_imag * margin).astype(BF16)


def pivot_inverse(pivot_h, pivot_s, shift_real, shift_imag):
    size = pivot_h.shape[0]
    margin = pivot_s.astype(F32)
    real = pivot_h.astype(F32) - shift_real * margin
    imag = -shift_imag * margin
    on_diagonal = lax.broadcasted_iota(jnp.int32, (size, size), 0) == lax.broadcasted_iota(
        jnp.int32, (size, size), 1
    )
    only_real = jnp.where(on_diagonal, real, 0.0)
    only_imag = jnp.where(on_diagonal, imag, 0.0)

    def start(axis):
        diag_real = jnp.sum(only_real, axis=axis, keepdims=True)
        diag_imag = jnp.sum(only_imag, axis=axis, keepdims=True)
        denom = diag_real * diag_real + diag_imag * diag_imag
        return diag_real / denom, -diag_imag / denom

    left_real, left_imag = start(1)
    right_real, right_imag = start(0)
    identity = jnp.where(on_diagonal, 1.0, 0.0)
    first = (
        identity - (left_real * real - left_imag * imag),
        -(left_real * imag + left_imag * real),
    )
    first_b = rounded(first)
    first_below = below(first_b)
    second = halves(nn(side(first_b), first_below))
    second_b = rounded(second)
    wide = nn(side(second_b), jnp.concatenate([first_below, below(second_b)], axis=1))
    third = halves(wide[:, : 2 * size])
    fourth_b = rounded(halves(wide[:, 2 * size :]))
    total = plus(plus((identity + first[0], first[1]), second), third)
    tall = nn(
        jnp.concatenate([side(fourth_b), side(rounded(total))], axis=0), below(fourth_b)
    )
    eighth_b = rounded(halves(tall[:size]))
    total = plus(total, halves(tall[size:]))
    total = plus(total, product(rounded(total), eighth_b))
    return (
        total[0] * right_real - total[1] * right_imag,
        total[0] * right_imag + total[1] * right_real,
    )


def step(
    rows,
    cols,
    poles,
    shift_hbm,
    weight_hbm,
    pattern_hbm,
    front_h,
    front_s,
    panel_h,
    panel_s,
    pivot_h,
    pivot_s,
    ancestor,
    schur_out,
    rows_out,
    pivot_out,
    shift,
    weight,
    pattern,
    piv_v,
    own_panel,
    own_front,
    far_panel,
    far_front,
    anc_v,
    schur_v,
    final_rows,
    final_piv,
    part_rows,
    part_piv,
    send_rows,
    send_piv,
    recv_rows,
    recv_piv,
    layer_send,
    layer_recv,
    pass_ssem,
    pass_rsem,
    local_sem,
    panel_ssem,
    panel_rsem,
    front_ssem,
    front_rsem,
    rows_ssem,
    rows_rsem,
    piv_ssem,
    piv_rsem,
    layer_ssem,
    layer_rsem,
    last_ssem,
    last_rsem,
    out_sem,
):
    row = lax.axis_index("row")
    col = lax.axis_index("col")
    pole = lax.axis_index("pole")
    layer = poles * cols
    me = pole * cols + col
    width = front_h.shape[0]
    block = panel_h.shape[0]
    size = pivot_h.shape[0]
    piece = size // poles
    strip = size // cols

    def row_peer(offset):
        return lax.rem(row + offset, rows)

    def layer_peer(offset):
        index = lax.rem(me + offset, layer)
        return index, {"pole": index // cols, "col": lax.rem(index, cols)}

    barrier = pltpu.get_barrier_semaphore()
    for offset in range(1, rows):
        pl.semaphore_signal(
            barrier, inc=1, device_id={"row": row_peer(offset)}, device_id_type=MESH
        )
    for offset in range(1, layer):
        pl.semaphore_signal(
            barrier, inc=1, device_id=layer_peer(offset)[1], device_id_type=MESH
        )

    here = pl.ds(pl.multiple_of(col * width, width), width)
    mine = pl.ds(pl.multiple_of(row * block, block), block)
    local = [
        pltpu.make_async_copy(source, target, local_sem.at[index])
        for index, (source, target) in enumerate(
            [
                (panel_h, own_panel.at[0]),
                (panel_s, own_panel.at[1]),
                (shift_hbm, shift),
                (pivot_h, piv_v.at[0]),
                (pivot_s, piv_v.at[1]),
                (front_h, own_front.at[0]),
                (front_s, own_front.at[1]),
                (weight_hbm, weight),
                (pattern_hbm, pattern),
                (ancestor, anc_v),
            ]
        )
    ]
    for copy in local:
        copy.start()
    pl.semaphore_wait(barrier, rows - 1 + layer - 1)
    for copy in local[:2]:
        copy.wait()

    shares = poles if width % (16 * poles) == 0 else 1
    height = width // shares
    first = pl.multiple_of(pole * height if shares > 1 else 0, height)
    held = pl.ds(first, height)
    source_rows = pl.ds(pl.multiple_of(col * width + first, height), height)
    panel_sends = []
    panel_recvs = []
    panel_passes = []
    passed_recvs = []
    front_sends = []
    front_recvs = []
    for offset in range(1, rows):
        to = row_peer(offset)
        origin = lax.rem(row + rows - offset, rows)
        for slot, group in ((row, panel_sends), (origin, panel_recvs)):
            group.append(
                pltpu.make_async_remote_copy(
                    src_ref=own_panel.at[:, source_rows],
                    dst_ref=far_panel.at[:, slot, held],
                    send_sem=panel_ssem.at[offset - 1],
                    recv_sem=panel_rsem.at[offset - 1],
                    device_id={"row": to},
                    device_id_type=MESH,
                )
            )
        for hop in range(1, shares):
            giver = lax.rem(pole + shares - hop, shares)
            theirs = pl.ds(pl.multiple_of(giver * height, height), height)
            for rows_of, group in ((held, panel_passes), (theirs, passed_recvs)):
                group.append(
                    pltpu.make_async_remote_copy(
                        src_ref=far_panel.at[:, origin, held],
                        dst_ref=far_panel.at[:, origin, rows_of],
                        send_sem=pass_ssem.at[offset - 1, hop - 1],
                        recv_sem=pass_rsem.at[offset - 1, hop - 1],
                        device_id={"pole": lax.rem(pole + hop, shares)},
                        device_id_type=MESH,
                    )
                )
        theirs = pl.ds(pl.multiple_of(to * block, block), block)
        for slot, group in ((row, front_sends), (origin, front_recvs)):
            group.append(
                pltpu.make_async_remote_copy(
                    src_ref=own_front.at[:, :, theirs],
                    dst_ref=far_front.at[:, slot],
                    send_sem=front_ssem.at[offset - 1],
                    recv_sem=front_rsem.at[offset - 1],
                    device_id={"row": to},
                    device_id_type=MESH,
                )
            )
    for copy in panel_sends:
        copy.start()

    for copy in local[2:5]:
        copy.wait()
    shift_real = shift[0, 0]
    shift_imag = shift[0, 1]
    inverse = pivot_inverse(piv_v[0], piv_v[1], shift_real, shift_imag)
    inv_high, inv_low = split(inverse)
    for copy in panel_recvs:
        copy.wait_recv()
    for copy in panel_passes:
        copy.start()
    for copy in panel_sends:
        copy.wait_send()
    for copy in local[5:]:
        copy.wait()
    for copy in front_sends:
        copy.start()
    far_panel[:, row] = own_panel[:, here]
    far_front[:, row] = own_front[:, :, mine]
    weight_real = weight[0, 0]
    weight_imag = weight[0, 1]
    coupling = couple(own_panel[0], own_panel[1], shift_real, shift_imag)
    coupling_across = across(coupling)
    flipped = rounded(
        halves(nt(side(inv_high), coupling_across) + nt(side(inv_low), coupling_across))
    )
    anc = (
        anc_v[0].reshape(rows * width, block),
        anc_v[1].reshape(rows * width, block),
    )
    swept = product_nt(flipped, anc)
    swept_both = side(
        rounded(
            (
                weight_real * swept[1] + weight_imag * swept[0],
                weight_real * swept[0] - weight_imag * swept[1],
            )
        )
    )
    own_share = (weight_real * inverse[1] + weight_imag * inverse[0]) * (1.0 / (rows * cols))
    anc_flipped = side((anc[0].T, anc[1].T))
    inv_below = jnp.concatenate([below(inv_high), below(inv_low)], axis=0)

    for copy in passed_recvs:
        copy.wait_recv()
    far_coupling = side(
        couple(
            far_panel[0].reshape(rows * width, size),
            far_panel[1].reshape(rows * width, size),
            shift_real,
            shift_imag,
        )
    )
    solved = rounded(halves(nn(jnp.concatenate([far_coupling, far_coupling], axis=1), inv_below)))

    def scatter(value, kept, sent, height):
        for index in range(layer):
            tile = value[
                (index % cols) * height : (index % cols + 1) * height,
                (index // cols) * piece : (index // cols + 1) * piece,
            ]
            kept[index] = tile
            sent[index] = tile.astype(BF16)

    def exchange(sent, received, ssem, rsem):
        copies = []
        for offset in range(1, layer):
            index, device = layer_peer(offset)
            copies.append(
                pltpu.make_async_remote_copy(
                    src_ref=sent.at[index],
                    dst_ref=received.at[offset - 1],
                    send_sem=ssem.at[offset - 1],
                    recv_sem=rsem.at[offset - 1],
                    device_id=device,
                    device_id_type=MESH,
                )
            )
        for copy in copies:
            copy.start()
        return copies

    share = own_share + nn(swept_both, jnp.concatenate(solved, axis=0))
    scatter(share, part_piv, send_piv, strip)
    piv_copies = exchange(send_piv, recv_piv, piv_ssem, piv_rsem)
    part = halves(nn(anc_flipped, below(solved)))
    weighted_imag = -(weight_real * part[1] + weight_imag * part[0])
    scatter(weighted_imag, part_rows, send_rows, width)

    update = halves(nt(side(solved), coupling_across))

    for copy in piv_copies:
        copy.wait_recv()
    layer_sum = part_piv[me]
    for offset in range(layer - 1):
        layer_sum = layer_sum + recv_piv[offset].astype(F32)
    layer_send[...] = layer_sum.astype(BF16)
    layer_copies = [
        pltpu.make_async_remote_copy(
            src_ref=layer_send,
            dst_ref=layer_recv.at[offset - 1],
            send_sem=layer_ssem.at[offset - 1],
            recv_sem=layer_rsem.at[offset - 1],
            device_id={"row": row_peer(offset)},
            device_id_type=MESH,
        )
        for offset in range(1, rows)
    ]
    for copy in layer_copies:
        copy.start()
    rows_copies = exchange(send_rows, recv_rows, rows_ssem, rows_rsem)

    for copy in layer_copies:
        copy.wait_recv()
    whole = layer_sum
    for offset in range(rows - 1):
        whole = whole + layer_recv[offset].astype(F32)
    final_piv[...] = whole
    own_copy = pltpu.make_async_copy(final_piv, pivot_out.at[col], out_sem.at[2])
    own_copy.start()
    last_copies = []
    last_recvs = []
    for offset in range(1, cols):
        to = lax.rem(col + offset, cols)
        origin = lax.rem(col + cols - offset, cols)
        for slot, group in ((col, last_copies), (origin, last_recvs)):
            group.append(
                pltpu.make_async_remote_copy(
                    src_ref=final_piv,
                    dst_ref=pivot_out.at[slot],
                    send_sem=last_ssem.at[offset - 1],
                    recv_sem=last_rsem.at[offset - 1],
                    device_id={"col": to},
                    device_id_type=MESH,
                )
            )
    for copy in last_copies:
        copy.start()

    for copy in front_recvs:
        copy.wait_recv()
    for index in range(rows):
        flag = pattern[index, row].astype(F32)
        margin = far_front[1, index].astype(F32)
        hamil = far_front[0, index].astype(F32)
        at = slice(index * width, (index + 1) * width)
        schur_v[0, index] = (flag * (hamil - shift_real * margin) - update[0][at]).astype(BF16)
        schur_v[1, index] = (flag * (-shift_imag * margin) - update[1][at]).astype(BF16)

    schur_copy = pltpu.make_async_copy(schur_v, schur_out, out_sem.at[0])
    schur_copy.start()

    for copy in rows_copies:
        copy.wait_recv()
    rows_sum = part_rows[me]
    for offset in range(layer - 1):
        rows_sum = rows_sum + recv_rows[offset].astype(F32)
    final_rows[...] = rows_sum
    rows_copy = pltpu.make_async_copy(final_rows, rows_out, out_sem.at[1])
    rows_copy.start()

    for copy in panel_passes + front_sends + piv_copies + layer_copies + rows_copies:
        copy.wait_send()
    schur_copy.wait()
    rows_copy.wait()
    own_copy.wait()
    for copy in last_copies:
        copy.wait_send()
    for copy in last_recvs:
        copy.wait_recv()


def hand_over(*refs):
    sources, targets, staged, sems = refs[:3], refs[3:6], refs[6:9], refs[9]
    inward = []
    outward = []
    for index in range(3):
        inward.append(
            pltpu.make_async_copy(sources[index], staged[index], sems.at[0, index])
        )
        outward.append(
            pltpu.make_async_copy(staged[index], targets[index], sems.at[1, index])
        )
        inward[index].start()
    for index in range(3):
        inward[index].wait()
        outward[index].start()
    for copy in outward:
        copy.wait()


def shards(
    rows,
    cols,
    poles,
    front_h,
    front_s,
    panel_h,
    panel_s,
    pivot_h,
    pivot_s,
    pole_shift,
    pole_weight,
    pattern,
    ancestor_inverse,
):
    width = front_h.shape[0]
    block = panel_h.shape[0]
    size = pivot_h.shape[0]
    piece = size // poles
    strip = size // cols
    layer = poles * cols
    ancestor = ancestor_inverse.reshape(2, rows, width, block)
    hbm = pl.BlockSpec(memory_space=pl.ANY)
    dma = pltpu.SemaphoreType.DMA
    out_shape = (
        jax.ShapeDtypeStruct((2, rows, width, block), BF16),
        jax.ShapeDtypeStruct((width, piece), F32),
        jax.ShapeDtypeStruct((cols, strip, piece), F32),
    )
    found = pl.pallas_call(
        functools.partial(step, rows, cols, poles),
        out_shape=out_shape,
        in_specs=[hbm] * 10,
        out_specs=(hbm,) * 3,
        scratch_shapes=[
            pltpu.SMEM(pole_shift.shape, F32),
            pltpu.SMEM(pole_weight.shape, F32),
            pltpu.SMEM(pattern.shape, jnp.int32),
            pltpu.VMEM((2, size, size), BF16),
            pltpu.VMEM((2, block, size), BF16),
            pltpu.VMEM((2,) + front_h.shape, BF16),
            pltpu.VMEM((2, rows, width, size), BF16),
            pltpu.VMEM((2, rows, width, block), BF16),
            pltpu.VMEM((2, rows, width, block), BF16),
            pltpu.VMEM((2, rows, width, block), BF16),
            pltpu.VMEM((width, piece), F32),
            pltpu.VMEM((strip, piece), F32),
            pltpu.VMEM((layer, width, piece), F32),
            pltpu.VMEM((layer, strip, piece), F32),
            pltpu.VMEM((layer, width, piece), BF16),
            pltpu.VMEM((layer, strip, piece), BF16),
            pltpu.VMEM((layer - 1, width, piece), BF16),
            pltpu.VMEM((layer - 1, strip, piece), BF16),
            pltpu.VMEM((strip, piece), BF16),
            pltpu.VMEM((rows - 1, strip, piece), BF16),
            dma((rows - 1, poles - 1)),
            dma((rows - 1, poles - 1)),
            dma((10,)),
            dma((rows - 1,)),
            dma((rows - 1,)),
            dma((rows - 1,)),
            dma((rows - 1,)),
            dma((layer - 1,)),
            dma((layer - 1,)),
            dma((layer - 1,)),
            dma((layer - 1,)),
            dma((rows - 1,)),
            dma((rows - 1,)),
            dma((cols - 1,)),
            dma((cols - 1,)),
            dma((3,)),
        ],
        compiler_params=pltpu.CompilerParams(
            collective_id=0, has_side_effects=True, vmem_limit_bytes=60 * 1024 * 1024
        ),
        name="front_step",
    )(
        pole_shift,
        pole_weight,
        pattern,
        front_h,
        front_s,
        panel_h,
        panel_s,
        pivot_h,
        pivot_s,
        ancestor,
    )
    schur, rows_out, pivot_out = pl.pallas_call(
        hand_over,
        out_shape=out_shape,
        in_specs=[hbm] * 3,
        out_specs=(hbm,) * 3,
        scratch_shapes=[pltpu.VMEM(part.shape, part.dtype) for part in out_shape]
        + [dma((2, 3))],
        compiler_params=pltpu.CompilerParams(vmem_limit_bytes=60 * 1024 * 1024),
        name="hand_over",
    )(*found)
    return (
        schur.reshape(ancestor_inverse.shape),
        rows_out,
        pivot_out.reshape(size, piece),
    )


def solution(mesh):
    sizes = dict(mesh.shape)
    in_specs = (
        P(("row", "col"), None),
        P(("row", "col"), None),
        P("row", None),
        P("row", None),
        P(),
        P(),
        P("pole", None),
        P("pole", None),
        P(),
        P("pole", None, None, "col", None, "row"),
    )
    out_specs = (
        P("pole", None, None, "col", None, "row"),
        P(("row", "col"), "pole"),
        P(None, "pole"),
    )
    body = functools.partial(shards, sizes["row"], sizes["col"], sizes["pole"])
    return jax.shard_map(body, mesh=mesh, in_specs=in_specs, out_specs=out_specs, check_vma=False)
```

```python
import functools

import jax
import jax.numpy as jnp
from jax import lax
from jax.experimental import pallas as pl
from jax.experimental.pallas import tpu as pltpu
from jax.sharding import PartitionSpec as P

MESH = pl.DeviceIdType.MESH
F32 = jnp.float32
BF16 = jnp.bfloat16


def nn(left, right):
    return lax.dot_general(left, right, (((1,), (0,)), ((), ())), preferred_element_type=F32)


def nt(left, right):
    return lax.dot_general(left, right, (((1,), (1,)), ((), ())), preferred_element_type=F32)


def side(pair):
    return jnp.concatenate(pair, axis=1)


def below(pair):
    real, imag = pair
    return jnp.concatenate([side((real, imag)), side((-imag, real))], axis=0)


def across(pair):
    real, imag = pair
    return jnp.concatenate([side((real, -imag)), side((imag, real))], axis=0)


def halves(value):
    middle = value.shape[1] // 2
    return value[:, :middle], value[:, middle:]


def product(left, right):
    return halves(nn(side(left), below(right)))


def rounded(pair):
    return pair[0].astype(BF16), pair[1].astype(BF16)


def split(pair):
    high = rounded(pair)
    low = rounded((pair[0] - high[0].astype(F32), pair[1] - high[1].astype(F32)))
    return high, low


def plus(left, right):
    return left[0] + right[0], left[1] + right[1]


def couple(rows_h, rows_s, shift_real, shift_imag):
    margin = rows_s.astype(F32)
    real = rows_h.astype(F32) - shift_real * margin
    return real.astype(BF16), (-shift_imag * margin).astype(BF16)


def pivot_inverse(pivot_h, pivot_s, shift_real, shift_imag, meanwhile):
    size = pivot_h.shape[0]
    margin = pivot_s.astype(F32)
    real = pivot_h.astype(F32) - shift_real * margin
    imag = -shift_imag * margin
    on_diagonal = lax.broadcasted_iota(jnp.int32, (size, size), 0) == lax.broadcasted_iota(
        jnp.int32, (size, size), 1
    )
    only_real = jnp.where(on_diagonal, real, 0.0)
    only_imag = jnp.where(on_diagonal, imag, 0.0)

    def start(axis):
        diag_real = jnp.sum(only_real, axis=axis, keepdims=True)
        diag_imag = jnp.sum(only_imag, axis=axis, keepdims=True)
        denom = diag_real * diag_real + diag_imag * diag_imag
        return diag_real / denom, -diag_imag / denom

    left_real, left_imag = start(1)
    right_real, right_imag = start(0)
    identity = jnp.where(on_diagonal, 1.0, 0.0)
    first = (
        identity - (left_real * real - left_imag * imag),
        -(left_real * imag + left_imag * real),
    )
    first_b = rounded(first)
    first_below = below(first_b)
    second = halves(nn(side(first_b), first_below))
    second_b = rounded(second)
    wide = nn(side(second_b), jnp.concatenate([first_below, below(second_b)], axis=1))
    third = halves(wide[:, : 2 * size])
    fourth_b = rounded(halves(wide[:, 2 * size :]))
    total = plus(plus((identity + first[0], first[1]), second), third)
    tall = nn(
        jnp.concatenate([side(fourth_b), side(rounded(total))], axis=0), below(fourth_b)
    )
    eighth_b = rounded(halves(tall[:size]))
    total = plus(total, halves(tall[size:]))
    meanwhile()
    total = plus(total, product(rounded(total), eighth_b))
    return (
        total[0] * right_real - total[1] * right_imag,
        total[0] * right_imag + total[1] * right_real,
    )


def step(
    rows,
    cols,
    poles,
    shift_hbm,
    weight_hbm,
    pattern_hbm,
    front_h,
    front_s,
    panel_h,
    panel_s,
    pivot_h,
    pivot_s,
    ancestor,
    schur_out,
    rows_out,
    pivot_out,
    shift,
    weight,
    pattern,
    piv_v,
    own_panel,
    own_front,
    far_panel,
    far_front,
    anc_v,
    schur_v,
    final_rows,
    final_piv,
    part_rows,
    part_piv,
    send_rows,
    send_piv,
    recv_rows,
    recv_piv,
    layer_send,
    layer_recv,
    pass_ssem,
    pass_rsem,
    local_sem,
    panel_ssem,
    panel_rsem,
    front_ssem,
    front_rsem,
    rows_ssem,
    rows_rsem,
    piv_ssem,
    piv_rsem,
    layer_ssem,
    layer_rsem,
    last_ssem,
    last_rsem,
    out_sem,
):
    row = lax.axis_index("row")
    col = lax.axis_index("col")
    pole = lax.axis_index("pole")
    layer = poles * cols
    me = pole * cols + col
    width = front_h.shape[0]
    block = panel_h.shape[0]
    size = pivot_h.shape[0]
    piece = size // poles
    strip = size // cols

    def row_peer(offset):
        return lax.rem(row + offset, rows)

    def layer_peer(offset):
        index = lax.rem(me + offset, layer)
        return index, {"pole": index // cols, "col": lax.rem(index, cols)}

    barrier = pltpu.get_barrier_semaphore()
    for offset in range(1, rows):
        pl.semaphore_signal(
            barrier, inc=1, device_id={"row": row_peer(offset)}, device_id_type=MESH
        )
    for offset in range(1, layer):
        pl.semaphore_signal(
            barrier, inc=1, device_id=layer_peer(offset)[1], device_id_type=MESH
        )

    here = pl.ds(pl.multiple_of(col * width, width), width)
    mine = pl.ds(pl.multiple_of(row * block, block), block)
    local = [
        pltpu.make_async_copy(source, target, local_sem.at[index])
        for index, (source, target) in enumerate(
            [
                (panel_h, own_panel.at[0]),
                (panel_s, own_panel.at[1]),
                (shift_hbm, shift),
                (pivot_h, piv_v.at[0]),
                (pivot_s, piv_v.at[1]),
                (front_h, own_front.at[0]),
                (front_s, own_front.at[1]),
                (weight_hbm, weight),
                (pattern_hbm, pattern),
                (ancestor, anc_v),
            ]
        )
    ]
    for copy in local:
        copy.start()
    pl.semaphore_wait(barrier, rows - 1 + layer - 1)
    for copy in local[:2]:
        copy.wait()

    shares = poles if width % (16 * poles) == 0 else 1
    height = width // shares
    first = pl.multiple_of(pole * height if shares > 1 else 0, height)
    held = pl.ds(first, height)
    source_rows = pl.ds(pl.multiple_of(col * width + first, height), height)
    panel_sends = []
    panel_recvs = []
    panel_passes = []
    passed_recvs = []
    front_sends = []
    front_recvs = []
    for offset in range(1, rows):
        to = row_peer(offset)
        origin = lax.rem(row + rows - offset, rows)
        for slot, group in ((row, panel_sends), (origin, panel_recvs)):
            group.append(
                pltpu.make_async_remote_copy(
                    src_ref=own_panel.at[:, source_rows],
                    dst_ref=far_panel.at[:, slot, held],
                    send_sem=panel_ssem.at[offset - 1],
                    recv_sem=panel_rsem.at[offset - 1],
                    device_id={"row": to},
                    device_id_type=MESH,
                )
            )
        for hop in range(1, shares):
            giver = lax.rem(pole + shares - hop, shares)
            theirs = pl.ds(pl.multiple_of(giver * height, height), height)
            for rows_of, group in ((held, panel_passes), (theirs, passed_recvs)):
                group.append(
                    pltpu.make_async_remote_copy(
                        src_ref=far_panel.at[:, origin, held],
                        dst_ref=far_panel.at[:, origin, rows_of],
                        send_sem=pass_ssem.at[offset - 1, hop - 1],
                        recv_sem=pass_rsem.at[offset - 1, hop - 1],
                        device_id={"pole": lax.rem(pole + hop, shares)},
                        device_id_type=MESH,
                    )
                )
        theirs = pl.ds(pl.multiple_of(to * block, block), block)
        for slot, group in ((row, front_sends), (origin, front_recvs)):
            group.append(
                pltpu.make_async_remote_copy(
                    src_ref=own_front.at[:, :, theirs],
                    dst_ref=far_front.at[:, slot],
                    send_sem=front_ssem.at[offset - 1],
                    recv_sem=front_rsem.at[offset - 1],
                    device_id={"row": to},
                    device_id_type=MESH,
                )
            )
    for copy in panel_sends:
        copy.start()

    for copy in local[2:5]:
        copy.wait()
    shift_real = shift[0, 0]
    shift_imag = shift[0, 1]

    def pass_on():
        for copy in panel_recvs:
            copy.wait_recv()
        for copy in panel_passes:
            copy.start()
        for copy in panel_sends:
            copy.wait_send()
        for copy in local[5:7]:
            copy.wait()
        for copy in front_sends:
            copy.start()

    inverse = pivot_inverse(piv_v[0], piv_v[1], shift_real, shift_imag, pass_on)
    inv_high, inv_low = split(inverse)
    inv_below = jnp.concatenate([below(inv_high), below(inv_low)], axis=0)
    for copy in local[7:]:
        copy.wait()
    weight_real = weight[0, 0]
    weight_imag = weight[0, 1]
    coupling = couple(own_panel[0], own_panel[1], shift_real, shift_imag)
    coupled = side(coupling)
    own_solved = rounded(halves(nn(side((coupled, coupled)), inv_below)))
    anc = (
        anc_v[0].reshape(rows * width, block),
        anc_v[1].reshape(rows * width, block),
    )
    swept = product(anc, own_solved)
    swept_imag = (weight_real * swept[1] + weight_imag * swept[0]).astype(BF16)
    swept_real = (weight_real * swept[0] - weight_imag * swept[1]).astype(BF16)
    swept_both = side((swept_imag.T, swept_real.T))
    own_share = (weight_real * inverse[1] + weight_imag * inverse[0]) * (1.0 / (rows * cols))
    far_panel[:, row] = own_panel[:, here]

    for copy in passed_recvs:
        copy.wait_recv()
    far_coupling = side(
        couple(
            far_panel[0].reshape(rows * width, size),
            far_panel[1].reshape(rows * width, size),
            shift_real,
            shift_imag,
        )
    )
    solved = rounded(halves(nn(jnp.concatenate([far_coupling, far_coupling], axis=1), inv_below)))

    def scatter(value, kept, sent, height):
        for index in range(layer):
            tile = value[
                (index % cols) * height : (index % cols + 1) * height,
                (index // cols) * piece : (index // cols + 1) * piece,
            ]
            kept[index] = tile
            sent[index] = tile.astype(BF16)

    def exchange(sent, received, ssem, rsem):
        copies = []
        for offset in range(1, layer):
            index, device = layer_peer(offset)
            copies.append(
                pltpu.make_async_remote_copy(
                    src_ref=sent.at[index],
                    dst_ref=received.at[offset - 1],
                    send_sem=ssem.at[offset - 1],
                    recv_sem=rsem.at[offset - 1],
                    device_id=device,
                    device_id_type=MESH,
                )
            )
        for copy in copies:
            copy.start()
        return copies

    share = own_share + nn(swept_both, jnp.concatenate(solved, axis=0))
    scatter(share, part_piv, send_piv, strip)
    piv_copies = exchange(send_piv, recv_piv, piv_ssem, piv_rsem)
    part = halves(nn(side((anc[0].T, anc[1].T)), below(solved)))
    weighted_imag = -(weight_real * part[1] + weight_imag * part[0])
    scatter(weighted_imag, part_rows, send_rows, width)

    update = halves(nt(side(solved), across(coupling)))
    far_front[:, row] = own_front[:, :, mine]

    for copy in piv_copies:
        copy.wait_recv()
    layer_sum = part_piv[me]
    for offset in range(layer - 1):
        layer_sum = layer_sum + recv_piv[offset].astype(F32)
    layer_send[...] = layer_sum.astype(BF16)
    layer_copies = [
        pltpu.make_async_remote_copy(
            src_ref=layer_send,
            dst_ref=layer_recv.at[offset - 1],
            send_sem=layer_ssem.at[offset - 1],
            recv_sem=layer_rsem.at[offset - 1],
            device_id={"row": row_peer(offset)},
            device_id_type=MESH,
        )
        for offset in range(1, rows)
    ]
    for copy in layer_copies:
        copy.start()
    rows_copies = exchange(send_rows, recv_rows, rows_ssem, rows_rsem)

    for copy in layer_copies:
        copy.wait_recv()
    whole = layer_sum
    for offset in range(rows - 1):
        whole = whole + layer_recv[offset].astype(F32)
    final_piv[...] = whole
    own_copy = pltpu.make_async_copy(final_piv, pivot_out.at[col], out_sem.at[2])
    own_copy.start()
    last_copies = []
    last_recvs = []
    for offset in range(1, cols):
        to = lax.rem(col + offset, cols)
        origin = lax.rem(col + cols - offset, cols)
        for slot, group in ((col, last_copies), (origin, last_recvs)):
            group.append(
                pltpu.make_async_remote_copy(
                    src_ref=final_piv,
                    dst_ref=pivot_out.at[slot],
                    send_sem=last_ssem.at[offset - 1],
                    recv_sem=last_rsem.at[offset - 1],
                    device_id={"col": to},
                    device_id_type=MESH,
                )
            )
    for copy in last_copies:
        copy.start()

    for copy in front_recvs:
        copy.wait_recv()
    for index in range(rows):
        flag = pattern[index, row].astype(F32)
        margin = far_front[1, index].astype(F32)
        hamil = far_front[0, index].astype(F32)
        at = slice(index * width, (index + 1) * width)
        schur_v[0, index] = (flag * (hamil - shift_real * margin) - update[0][at]).astype(BF16)
        schur_v[1, index] = (flag * (-shift_imag * margin) - update[1][at]).astype(BF16)

    schur_copy = pltpu.make_async_copy(schur_v, schur_out, out_sem.at[0])
    schur_copy.start()

    for copy in rows_copies:
        copy.wait_recv()
    rows_sum = part_rows[me]
    for offset in range(layer - 1):
        rows_sum = rows_sum + recv_rows[offset].astype(F32)
    final_rows[...] = rows_sum
    rows_copy = pltpu.make_async_copy(final_rows, rows_out, out_sem.at[1])
    rows_copy.start()

    for copy in panel_passes + front_sends + piv_copies + layer_copies + rows_copies:
        copy.wait_send()
    schur_copy.wait()
    rows_copy.wait()
    own_copy.wait()
    for copy in last_copies:
        copy.wait_send()
    for copy in last_recvs:
        copy.wait_recv()


def hand_over(*refs):
    sources, targets, staged, sems = refs[:3], refs[3:6], refs[6:9], refs[9]
    inward = []
    outward = []
    for index in range(3):
        inward.append(
            pltpu.make_async_copy(sources[index], staged[index], sems.at[0, index])
        )
        outward.append(
            pltpu.make_async_copy(staged[index], targets[index], sems.at[1, index])
        )
        inward[index].start()
    for index in range(3):
        inward[index].wait()
        outward[index].start()
    for copy in outward:
        copy.wait()


def shards(
    rows,
    cols,
    poles,
    front_h,
    front_s,
    panel_h,
    panel_s,
    pivot_h,
    pivot_s,
    pole_shift,
    pole_weight,
    pattern,
    ancestor_inverse,
):
    width = front_h.shape[0]
    block = panel_h.shape[0]
    size = pivot_h.shape[0]
    piece = size // poles
    strip = size // cols
    layer = poles * cols
    ancestor = ancestor_inverse.reshape(2, rows, width, block)
    hbm = pl.BlockSpec(memory_space=pl.ANY)
    dma = pltpu.SemaphoreType.DMA
    out_shape = (
        jax.ShapeDtypeStruct((2, rows, width, block), BF16),
        jax.ShapeDtypeStruct((width, piece), F32),
        jax.ShapeDtypeStruct((cols, strip, piece), F32),
    )
    found = pl.pallas_call(
        functools.partial(step, rows, cols, poles),
        out_shape=out_shape,
        in_specs=[hbm] * 10,
        out_specs=(hbm,) * 3,
        scratch_shapes=[
            pltpu.SMEM(pole_shift.shape, F32),
            pltpu.SMEM(pole_weight.shape, F32),
            pltpu.SMEM(pattern.shape, jnp.int32),
            pltpu.VMEM((2, size, size), BF16),
            pltpu.VMEM((2, block, size), BF16),
            pltpu.VMEM((2,) + front_h.shape, BF16),
            pltpu.VMEM((2, rows, width, size), BF16),
            pltpu.VMEM((2, rows, width, block), BF16),
            pltpu.VMEM((2, rows, width, block), BF16),
            pltpu.VMEM((2, rows, width, block), BF16),
            pltpu.VMEM((width, piece), F32),
            pltpu.VMEM((strip, piece), F32),
            pltpu.VMEM((layer, width, piece), F32),
            pltpu.VMEM((layer, strip, piece), F32),
            pltpu.VMEM((layer, width, piece), BF16),
            pltpu.VMEM((layer, strip, piece), BF16),
            pltpu.VMEM((layer - 1, width, piece), BF16),
            pltpu.VMEM((layer - 1, strip, piece), BF16),
            pltpu.VMEM((strip, piece), BF16),
            pltpu.VMEM((rows - 1, strip, piece), BF16),
            dma((rows - 1, poles - 1)),
            dma((rows - 1, poles - 1)),
            dma((10,)),
            dma((rows - 1,)),
            dma((rows - 1,)),
            dma((rows - 1,)),
            dma((rows - 1,)),
            dma((layer - 1,)),
            dma((layer - 1,)),
            dma((layer - 1,)),
            dma((layer - 1,)),
            dma((rows - 1,)),
            dma((rows - 1,)),
            dma((cols - 1,)),
            dma((cols - 1,)),
            dma((3,)),
        ],
        compiler_params=pltpu.CompilerParams(
            collective_id=0, has_side_effects=True, vmem_limit_bytes=60 * 1024 * 1024
        ),
        name="front_step",
    )(
        pole_shift,
        pole_weight,
        pattern,
        front_h,
        front_s,
        panel_h,
        panel_s,
        pivot_h,
        pivot_s,
        ancestor,
    )
    schur, rows_out, pivot_out = pl.pallas_call(
        hand_over,
        out_shape=out_shape,
        in_specs=[hbm] * 3,
        out_specs=(hbm,) * 3,
        scratch_shapes=[pltpu.VMEM(part.shape, part.dtype) for part in out_shape]
        + [dma((2, 3))],
        compiler_params=pltpu.CompilerParams(vmem_limit_bytes=60 * 1024 * 1024),
        name="hand_over",
    )(*found)
    return (
        schur.reshape(ancestor_inverse.shape),
        rows_out,
        pivot_out.reshape(size, piece),
    )


def solution(mesh):
    sizes = dict(mesh.shape)
    in_specs = (
        P(("row", "col"), None),
        P(("row", "col"), None),
        P("row", None),
        P("row", None),
        P(),
        P(),
        P("pole", None),
        P("pole", None),
        P(),
        P("pole", None, None, "col", None, "row"),
    )
    out_specs = (
        P("pole", None, None, "col", None, "row"),
        P(("row", "col"), "pole"),
        P(None, "pole"),
    )
    body = functools.partial(shards, sizes["row"], sizes["col"], sizes["pole"])
    return jax.shard_map(body, mesh=mesh, in_specs=in_specs, out_specs=out_specs, check_vma=False)
```

```python
import functools

import jax
import jax.numpy as jnp
from jax import lax
from jax.experimental import pallas as pl
from jax.experimental.pallas import tpu as pltpu
from jax.sharding import PartitionSpec as P

MESH = pl.DeviceIdType.MESH
F32 = jnp.float32
BF16 = jnp.bfloat16


def nn(left, right):
    return lax.dot_general(left, right, (((1,), (0,)), ((), ())), preferred_element_type=F32)


def nt(left, right):
    return lax.dot_general(left, right, (((1,), (1,)), ((), ())), preferred_element_type=F32)


def side(pair):
    return jnp.concatenate(pair, axis=1)


def below(pair):
    real, imag = pair
    return jnp.concatenate([side((real, imag)), side((-imag, real))], axis=0)


def across(pair):
    real, imag = pair
    return jnp.concatenate([side((real, -imag)), side((imag, real))], axis=0)


def halves(value):
    middle = value.shape[1] // 2
    return value[:, :middle], value[:, middle:]


def product(left, right):
    return halves(nn(side(left), below(right)))


def rounded(pair):
    return pair[0].astype(BF16), pair[1].astype(BF16)


def split(pair):
    high = rounded(pair)
    low = rounded((pair[0] - high[0].astype(F32), pair[1] - high[1].astype(F32)))
    return high, low


def plus(left, right):
    return left[0] + right[0], left[1] + right[1]


def couple(rows_h, rows_s, shift_real, shift_imag):
    margin = rows_s.astype(F32)
    real = rows_h.astype(F32) - shift_real * margin
    return real.astype(BF16), (-shift_imag * margin).astype(BF16)


def pivot_inverse(pivot_h, pivot_s, shift_real, shift_imag, meanwhile):
    size = pivot_h.shape[0]
    margin = pivot_s.astype(F32)
    real = pivot_h.astype(F32) - shift_real * margin
    imag = -shift_imag * margin
    on_diagonal = lax.broadcasted_iota(jnp.int32, (size, size), 0) == lax.broadcasted_iota(
        jnp.int32, (size, size), 1
    )
    only_real = jnp.where(on_diagonal, real, 0.0)
    only_imag = jnp.where(on_diagonal, imag, 0.0)

    def start(axis):
        diag_real = jnp.sum(only_real, axis=axis, keepdims=True)
        diag_imag = jnp.sum(only_imag, axis=axis, keepdims=True)
        denom = diag_real * diag_real + diag_imag * diag_imag
        return diag_real / denom, -diag_imag / denom

    left_real, left_imag = start(1)
    right_real, right_imag = start(0)
    identity = jnp.where(on_diagonal, 1.0, 0.0)
    first = (
        identity - (left_real * real - left_imag * imag),
        -(left_real * imag + left_imag * real),
    )
    first_b = rounded(first)
    first_below = below(first_b)
    second = halves(nn(side(first_b), first_below))
    second_b = rounded(second)
    wide = nn(side(second_b), jnp.concatenate([first_below, below(second_b)], axis=1))
    third = halves(wide[:, : 2 * size])
    fourth_b = rounded(halves(wide[:, 2 * size :]))
    total = plus(plus((identity + first[0], first[1]), second), third)
    tall = nn(
        jnp.concatenate([side(fourth_b), side(rounded(total))], axis=0), below(fourth_b)
    )
    eighth_b = rounded(halves(tall[:size]))
    total = plus(total, halves(tall[size:]))
    meanwhile()
    total = plus(total, product(rounded(total), eighth_b))
    return (
        total[0] * right_real - total[1] * right_imag,
        total[0] * right_imag + total[1] * right_real,
    )


def step(
    rows,
    cols,
    poles,
    shift_hbm,
    weight_hbm,
    pattern_hbm,
    front_h,
    front_s,
    panel_h,
    panel_s,
    pivot_h,
    pivot_s,
    ancestor,
    schur_out,
    rows_out,
    pivot_out,
    shift,
    weight,
    pattern,
    piv_v,
    own_panel,
    own_front,
    far_panel,
    far_front,
    anc_v,
    schur_v,
    final_rows,
    final_piv,
    part_rows,
    part_piv,
    send_rows,
    send_piv,
    recv_rows,
    recv_piv,
    layer_send,
    layer_recv,
    pass_ssem,
    pass_rsem,
    move_ssem,
    move_rsem,
    local_sem,
    panel_ssem,
    panel_rsem,
    front_ssem,
    front_rsem,
    rows_ssem,
    rows_rsem,
    piv_ssem,
    piv_rsem,
    layer_ssem,
    layer_rsem,
    last_ssem,
    last_rsem,
    out_sem,
):
    row = lax.axis_index("row")
    col = lax.axis_index("col")
    pole = lax.axis_index("pole")
    layer = poles * cols
    me = pole * cols + col
    width = front_h.shape[0]
    block = panel_h.shape[0]
    size = pivot_h.shape[0]
    piece = size // poles
    strip = size // cols

    def row_peer(offset):
        return lax.rem(row + offset, rows)

    def layer_peer(offset):
        index = lax.rem(me + offset, layer)
        return index, {"pole": index // cols, "col": lax.rem(index, cols)}

    barrier = pltpu.get_barrier_semaphore()
    for offset in range(1, rows):
        pl.semaphore_signal(
            barrier, inc=1, device_id={"row": row_peer(offset)}, device_id_type=MESH
        )
    for offset in range(1, layer):
        pl.semaphore_signal(
            barrier, inc=1, device_id=layer_peer(offset)[1], device_id_type=MESH
        )

    here = pl.ds(pl.multiple_of(col * width, width), width)
    mine = pl.ds(pl.multiple_of(row * block, block), block)
    local = [
        pltpu.make_async_copy(source, target, local_sem.at[index])
        for index, (source, target) in enumerate(
            [
                (panel_h, own_panel.at[0]),
                (panel_s, own_panel.at[1]),
                (shift_hbm, shift),
                (pivot_h, piv_v.at[0]),
                (pivot_s, piv_v.at[1]),
                (front_h, own_front.at[0]),
                (front_s, own_front.at[1]),
                (weight_hbm, weight),
                (pattern_hbm, pattern),
                (ancestor, anc_v),
            ]
        )
    ]
    for copy in local:
        copy.start()
    pl.semaphore_wait(barrier, rows - 1 + layer - 1)
    for copy in local[:2]:
        copy.wait()

    shares = poles if width % (16 * poles) == 0 else 1
    height = width // shares
    first = pl.multiple_of(pole * height if shares > 1 else 0, height)
    held = pl.ds(first, height)
    source_rows = pl.ds(pl.multiple_of(col * width + first, height), height)
    panel_sends = []
    panel_recvs = []
    panel_passes = []
    passed_recvs = []
    front_passes = []
    moved_recvs = []
    front_sends = []
    front_recvs = []
    for offset in range(1, rows):
        to = row_peer(offset)
        origin = lax.rem(row + rows - offset, rows)
        for slot, group in ((row, panel_sends), (origin, panel_recvs)):
            group.append(
                pltpu.make_async_remote_copy(
                    src_ref=own_panel.at[:, source_rows],
                    dst_ref=far_panel.at[:, slot, held],
                    send_sem=panel_ssem.at[offset - 1],
                    recv_sem=panel_rsem.at[offset - 1],
                    device_id={"row": to},
                    device_id_type=MESH,
                )
            )
        for hop in range(1, shares):
            giver = lax.rem(pole + shares - hop, shares)
            theirs = pl.ds(pl.multiple_of(giver * height, height), height)
            for array, ssem, rsem, sends, recvs in (
                (far_panel, pass_ssem, pass_rsem, panel_passes, passed_recvs),
                (far_front, move_ssem, move_rsem, front_passes, moved_recvs),
            ):
                for rows_of, group in ((held, sends), (theirs, recvs)):
                    group.append(
                        pltpu.make_async_remote_copy(
                            src_ref=array.at[:, origin, held],
                            dst_ref=array.at[:, origin, rows_of],
                            send_sem=ssem.at[offset - 1, hop - 1],
                            recv_sem=rsem.at[offset - 1, hop - 1],
                            device_id={"pole": lax.rem(pole + hop, shares)},
                            device_id_type=MESH,
                        )
                    )
        theirs = pl.ds(pl.multiple_of(to * block, block), block)
        for slot, group in ((row, front_sends), (origin, front_recvs)):
            group.append(
                pltpu.make_async_remote_copy(
                    src_ref=own_front.at[:, held, theirs],
                    dst_ref=far_front.at[:, slot, held],
                    send_sem=front_ssem.at[offset - 1],
                    recv_sem=front_rsem.at[offset - 1],
                    device_id={"row": to},
                    device_id_type=MESH,
                )
            )
    for copy in panel_sends:
        copy.start()

    for copy in local[2:5]:
        copy.wait()
    shift_real = shift[0, 0]
    shift_imag = shift[0, 1]

    def pass_on():
        for copy in panel_recvs:
            copy.wait_recv()
        for copy in panel_passes:
            copy.start()
        for copy in panel_sends:
            copy.wait_send()
        for copy in local[5:7]:
            copy.wait()
        for copy in front_sends:
            copy.start()

    inverse = pivot_inverse(piv_v[0], piv_v[1], shift_real, shift_imag, pass_on)
    inv_high, inv_low = split(inverse)
    inv_below = jnp.concatenate([below(inv_high), below(inv_low)], axis=0)
    for copy in local[7:]:
        copy.wait()
    weight_real = weight[0, 0]
    weight_imag = weight[0, 1]
    coupling = couple(own_panel[0], own_panel[1], shift_real, shift_imag)
    coupled = side(coupling)
    own_solved = rounded(halves(nn(side((coupled, coupled)), inv_below)))
    anc = (
        anc_v[0].reshape(rows * width, block),
        anc_v[1].reshape(rows * width, block),
    )
    swept = product(anc, own_solved)
    swept_imag = (weight_real * swept[1] + weight_imag * swept[0]).astype(BF16)
    swept_real = (weight_real * swept[0] - weight_imag * swept[1]).astype(BF16)
    swept_both = side((swept_imag.T, swept_real.T))
    own_share = (weight_real * inverse[1] + weight_imag * inverse[0]) * (1.0 / (rows * cols))
    far_panel[:, row] = own_panel[:, here]

    for copy in passed_recvs:
        copy.wait_recv()
    far_coupling = side(
        couple(
            far_panel[0].reshape(rows * width, size),
            far_panel[1].reshape(rows * width, size),
            shift_real,
            shift_imag,
        )
    )
    solved = rounded(halves(nn(jnp.concatenate([far_coupling, far_coupling], axis=1), inv_below)))

    def scatter(value, kept, sent, height):
        for index in range(layer):
            tile = value[
                (index % cols) * height : (index % cols + 1) * height,
                (index // cols) * piece : (index // cols + 1) * piece,
            ]
            kept[index] = tile
            sent[index] = tile.astype(BF16)

    def exchange(sent, received, ssem, rsem):
        copies = []
        for offset in range(1, layer):
            index, device = layer_peer(offset)
            copies.append(
                pltpu.make_async_remote_copy(
                    src_ref=sent.at[index],
                    dst_ref=received.at[offset - 1],
                    send_sem=ssem.at[offset - 1],
                    recv_sem=rsem.at[offset - 1],
                    device_id=device,
                    device_id_type=MESH,
                )
            )
        for copy in copies:
            copy.start()
        return copies

    share = own_share + nn(swept_both, jnp.concatenate(solved, axis=0))
    scatter(share, part_piv, send_piv, strip)
    piv_copies = exchange(send_piv, recv_piv, piv_ssem, piv_rsem)
    part = halves(nn(side((anc[0].T, anc[1].T)), below(solved)))
    weighted_imag = -(weight_real * part[1] + weight_imag * part[0])
    scatter(weighted_imag, part_rows, send_rows, width)

    update = halves(nt(side(solved), across(coupling)))
    far_front[:, row] = own_front[:, :, mine]

    for copy in piv_copies:
        copy.wait_recv()
    layer_sum = part_piv[me]
    for offset in range(layer - 1):
        layer_sum = layer_sum + recv_piv[offset].astype(F32)
    layer_send[...] = layer_sum.astype(BF16)
    layer_copies = [
        pltpu.make_async_remote_copy(
            src_ref=layer_send,
            dst_ref=layer_recv.at[offset - 1],
            send_sem=layer_ssem.at[offset - 1],
            recv_sem=layer_rsem.at[offset - 1],
            device_id={"row": row_peer(offset)},
            device_id_type=MESH,
        )
        for offset in range(1, rows)
    ]
    for copy in layer_copies:
        copy.start()
    for copy in front_recvs:
        copy.wait_recv()
    for copy in front_passes:
        copy.start()
    rows_copies = exchange(send_rows, recv_rows, rows_ssem, rows_rsem)

    for copy in layer_copies:
        copy.wait_recv()
    whole = layer_sum
    for offset in range(rows - 1):
        whole = whole + layer_recv[offset].astype(F32)
    final_piv[...] = whole
    own_copy = pltpu.make_async_copy(final_piv, pivot_out.at[col], out_sem.at[2])
    own_copy.start()
    last_copies = []
    last_recvs = []
    for offset in range(1, cols):
        to = lax.rem(col + offset, cols)
        origin = lax.rem(col + cols - offset, cols)
        for slot, group in ((col, last_copies), (origin, last_recvs)):
            group.append(
                pltpu.make_async_remote_copy(
                    src_ref=final_piv,
                    dst_ref=pivot_out.at[slot],
                    send_sem=last_ssem.at[offset - 1],
                    recv_sem=last_rsem.at[offset - 1],
                    device_id={"col": to},
                    device_id_type=MESH,
                )
            )
    for copy in last_copies:
        copy.start()

    for copy in moved_recvs:
        copy.wait_recv()
    for index in range(rows):
        flag = pattern[index, row].astype(F32)
        margin = far_front[1, index].astype(F32)
        hamil = far_front[0, index].astype(F32)
        at = slice(index * width, (index + 1) * width)
        schur_v[0, index] = (flag * (hamil - shift_real * margin) - update[0][at]).astype(BF16)
        schur_v[1, index] = (flag * (-shift_imag * margin) - update[1][at]).astype(BF16)

    schur_copy = pltpu.make_async_copy(schur_v, schur_out, out_sem.at[0])
    schur_copy.start()

    for copy in rows_copies:
        copy.wait_recv()
    rows_sum = part_rows[me]
    for offset in range(layer - 1):
        rows_sum = rows_sum + recv_rows[offset].astype(F32)
    final_rows[...] = rows_sum
    rows_copy = pltpu.make_async_copy(final_rows, rows_out, out_sem.at[1])
    rows_copy.start()

    for copy in panel_passes + front_sends + front_passes + piv_copies + layer_copies + rows_copies:
        copy.wait_send()
    schur_copy.wait()
    rows_copy.wait()
    own_copy.wait()
    for copy in last_copies:
        copy.wait_send()
    for copy in last_recvs:
        copy.wait_recv()


def hand_over(*refs):
    sources, targets, staged, sems = refs[:3], refs[3:6], refs[6:9], refs[9]
    inward = []
    outward = []
    for index in range(3):
        inward.append(
            pltpu.make_async_copy(sources[index], staged[index], sems.at[0, index])
        )
        outward.append(
            pltpu.make_async_copy(staged[index], targets[index], sems.at[1, index])
        )
        inward[index].start()
    for index in range(3):
        inward[index].wait()
        outward[index].start()
    for copy in outward:
        copy.wait()


def shards(
    rows,
    cols,
    poles,
    front_h,
    front_s,
    panel_h,
    panel_s,
    pivot_h,
    pivot_s,
    pole_shift,
    pole_weight,
    pattern,
    ancestor_inverse,
):
    width = front_h.shape[0]
    block = panel_h.shape[0]
    size = pivot_h.shape[0]
    piece = size // poles
    strip = size // cols
    layer = poles * cols
    ancestor = ancestor_inverse.reshape(2, rows, width, block)
    hbm = pl.BlockSpec(memory_space=pl.ANY)
    dma = pltpu.SemaphoreType.DMA
    out_shape = (
        jax.ShapeDtypeStruct((2, rows, width, block), BF16),
        jax.ShapeDtypeStruct((width, piece), F32),
        jax.ShapeDtypeStruct((cols, strip, piece), F32),
    )
    found = pl.pallas_call(
        functools.partial(step, rows, cols, poles),
        out_shape=out_shape,
        in_specs=[hbm] * 10,
        out_specs=(hbm,) * 3,
        scratch_shapes=[
            pltpu.SMEM(pole_shift.shape, F32),
            pltpu.SMEM(pole_weight.shape, F32),
            pltpu.SMEM(pattern.shape, jnp.int32),
            pltpu.VMEM((2, size, size), BF16),
            pltpu.VMEM((2, block, size), BF16),
            pltpu.VMEM((2,) + front_h.shape, BF16),
            pltpu.VMEM((2, rows, width, size), BF16),
            pltpu.VMEM((2, rows, width, block), BF16),
            pltpu.VMEM((2, rows, width, block), BF16),
            pltpu.VMEM((2, rows, width, block), BF16),
            pltpu.VMEM((width, piece), F32),
            pltpu.VMEM((strip, piece), F32),
            pltpu.VMEM((layer, width, piece), F32),
            pltpu.VMEM((layer, strip, piece), F32),
            pltpu.VMEM((layer, width, piece), BF16),
            pltpu.VMEM((layer, strip, piece), BF16),
            pltpu.VMEM((layer - 1, width, piece), BF16),
            pltpu.VMEM((layer - 1, strip, piece), BF16),
            pltpu.VMEM((strip, piece), BF16),
            pltpu.VMEM((rows - 1, strip, piece), BF16),
            dma((rows - 1, poles - 1)),
            dma((rows - 1, poles - 1)),
            dma((rows - 1, poles - 1)),
            dma((rows - 1, poles - 1)),
            dma((10,)),
            dma((rows - 1,)),
            dma((rows - 1,)),
            dma((rows - 1,)),
            dma((rows - 1,)),
            dma((layer - 1,)),
            dma((layer - 1,)),
            dma((layer - 1,)),
            dma((layer - 1,)),
            dma((rows - 1,)),
            dma((rows - 1,)),
            dma((cols - 1,)),
            dma((cols - 1,)),
            dma((3,)),
        ],
        compiler_params=pltpu.CompilerParams(
            collective_id=0, has_side_effects=True, vmem_limit_bytes=60 * 1024 * 1024
        ),
        name="front_step",
    )(
        pole_shift,
        pole_weight,
        pattern,
        front_h,
        front_s,
        panel_h,
        panel_s,
        pivot_h,
        pivot_s,
        ancestor,
    )
    schur, rows_out, pivot_out = pl.pallas_call(
        hand_over,
        out_shape=out_shape,
        in_specs=[hbm] * 3,
        out_specs=(hbm,) * 3,
        scratch_shapes=[pltpu.VMEM(part.shape, part.dtype) for part in out_shape]
        + [dma((2, 3))],
        compiler_params=pltpu.CompilerParams(vmem_limit_bytes=60 * 1024 * 1024),
        name="hand_over",
    )(*found)
    return (
        schur.reshape(ancestor_inverse.shape),
        rows_out,
        pivot_out.reshape(size, piece),
    )


def solution(mesh):
    sizes = dict(mesh.shape)
    in_specs = (
        P(("row", "col"), None),
        P(("row", "col"), None),
        P("row", None),
        P("row", None),
        P(),
        P(),
        P("pole", None),
        P("pole", None),
        P(),
        P("pole", None, None, "col", None, "row"),
    )
    out_specs = (
        P("pole", None, None, "col", None, "row"),
        P(("row", "col"), "pole"),
        P(None, "pole"),
    )
    body = functools.partial(shards, sizes["row"], sizes["col"], sizes["pole"])
    return jax.shard_map(body, mesh=mesh, in_specs=in_specs, out_specs=out_specs, check_vma=False)
```

```python
import functools

import jax
import jax.numpy as jnp
from jax import lax
from jax.experimental import pallas as pl
from jax.experimental.pallas import tpu as pltpu
from jax.sharding import PartitionSpec as P

MESH = pl.DeviceIdType.MESH
F32 = jnp.float32
BF16 = jnp.bfloat16


def nn(left, right):
    return lax.dot_general(left, right, (((1,), (0,)), ((), ())), preferred_element_type=F32)


def nt(left, right):
    return lax.dot_general(left, right, (((1,), (1,)), ((), ())), preferred_element_type=F32)


def side(pair):
    return jnp.concatenate(pair, axis=1)


def below(pair):
    real, imag = pair
    return jnp.concatenate([side((real, imag)), side((-imag, real))], axis=0)


def across(pair):
    real, imag = pair
    return jnp.concatenate([side((real, -imag)), side((imag, real))], axis=0)


def halves(value):
    middle = value.shape[1] // 2
    return value[:, :middle], value[:, middle:]


def product(left, right):
    return halves(nn(side(left), below(right)))


def rounded(pair):
    return pair[0].astype(BF16), pair[1].astype(BF16)


def split(pair):
    high = rounded(pair)
    low = rounded((pair[0] - high[0].astype(F32), pair[1] - high[1].astype(F32)))
    return high, low


def plus(left, right):
    return left[0] + right[0], left[1] + right[1]


def couple(rows_h, rows_s, shift_real, shift_imag):
    margin = rows_s.astype(F32)
    real = rows_h.astype(F32) - shift_real * margin
    return real.astype(BF16), (-shift_imag * margin).astype(BF16)


def pivot_inverse(pivot_h, pivot_s, shift_real, shift_imag, meanwhile):
    size = pivot_h.shape[0]
    margin = pivot_s.astype(F32)
    real = pivot_h.astype(F32) - shift_real * margin
    imag = -shift_imag * margin
    on_diagonal = lax.broadcasted_iota(jnp.int32, (size, size), 0) == lax.broadcasted_iota(
        jnp.int32, (size, size), 1
    )
    only_real = jnp.where(on_diagonal, real, 0.0)
    only_imag = jnp.where(on_diagonal, imag, 0.0)

    def start(axis):
        diag_real = jnp.sum(only_real, axis=axis, keepdims=True)
        diag_imag = jnp.sum(only_imag, axis=axis, keepdims=True)
        denom = diag_real * diag_real + diag_imag * diag_imag
        return diag_real / denom, -diag_imag / denom

    left_real, left_imag = start(1)
    right_real, right_imag = start(0)
    identity = jnp.where(on_diagonal, 1.0, 0.0)
    first = (
        identity - (left_real * real - left_imag * imag),
        -(left_real * imag + left_imag * real),
    )
    first_b = rounded(first)
    first_below = below(first_b)
    second = halves(nn(side(first_b), first_below))
    second_b = rounded(second)
    wide = nn(side(second_b), jnp.concatenate([first_below, below(second_b)], axis=1))
    third = halves(wide[:, : 2 * size])
    fourth_b = rounded(halves(wide[:, 2 * size :]))
    total = plus(plus((identity + first[0], first[1]), second), third)
    tall = nn(
        jnp.concatenate([side(fourth_b), side(rounded(total))], axis=0), below(fourth_b)
    )
    eighth_b = rounded(halves(tall[:size]))
    total = plus(total, halves(tall[size:]))
    meanwhile()
    total = plus(total, product(rounded(total), eighth_b))
    return (
        total[0] * right_real - total[1] * right_imag,
        total[0] * right_imag + total[1] * right_real,
    )


def step(
    rows,
    cols,
    poles,
    shift_hbm,
    weight_hbm,
    pattern_hbm,
    front_h,
    front_s,
    panel_h,
    panel_s,
    pivot_h,
    pivot_s,
    ancestor,
    schur_out,
    rows_out,
    pivot_out,
    shift,
    weight,
    pattern,
    piv_v,
    own_panel,
    own_front,
    far_panel,
    far_front,
    anc_v,
    schur_v,
    final_rows,
    final_piv,
    part_rows,
    part_piv,
    send_rows,
    send_piv,
    recv_rows,
    recv_piv,
    layer_send,
    layer_recv,
    pass_ssem,
    pass_rsem,
    local_sem,
    panel_ssem,
    panel_rsem,
    front_ssem,
    front_rsem,
    rows_ssem,
    rows_rsem,
    piv_ssem,
    piv_rsem,
    layer_ssem,
    layer_rsem,
    last_ssem,
    last_rsem,
    out_sem,
):
    row = lax.axis_index("row")
    col = lax.axis_index("col")
    pole = lax.axis_index("pole")
    layer = poles * cols
    me = pole * cols + col
    width = front_h.shape[0]
    block = panel_h.shape[0]
    size = pivot_h.shape[0]
    piece = size // poles
    strip = size // cols

    def row_peer(offset):
        return lax.rem(row + offset, rows)

    def layer_peer(offset):
        index = lax.rem(me + offset, layer)
        return index, {"pole": index // cols, "col": lax.rem(index, cols)}

    barrier = pltpu.get_barrier_semaphore()
    for offset in range(1, rows):
        pl.semaphore_signal(
            barrier, inc=1, device_id={"row": row_peer(offset)}, device_id_type=MESH
        )
    for offset in range(1, layer):
        pl.semaphore_signal(
            barrier, inc=1, device_id=layer_peer(offset)[1], device_id_type=MESH
        )

    here = pl.ds(pl.multiple_of(col * width, width), width)
    mine = pl.ds(pl.multiple_of(row * block, block), block)
    local = [
        pltpu.make_async_copy(source, target, local_sem.at[index])
        for index, (source, target) in enumerate(
            [
                (panel_h, own_panel.at[0]),
                (panel_s, own_panel.at[1]),
                (shift_hbm, shift),
                (pivot_h, piv_v.at[0]),
                (pivot_s, piv_v.at[1]),
                (front_h, own_front.at[0]),
                (front_s, own_front.at[1]),
                (weight_hbm, weight),
                (pattern_hbm, pattern),
                (ancestor, anc_v),
            ]
        )
    ]
    for copy in local:
        copy.start()
    pl.semaphore_wait(barrier, rows - 1 + layer - 1)
    for copy in local[:2]:
        copy.wait()

    shares = poles if width % (16 * poles) == 0 else 1
    height = width // shares
    first = pl.multiple_of(pole * height if shares > 1 else 0, height)
    held = pl.ds(first, height)
    source_rows = pl.ds(pl.multiple_of(col * width + first, height), height)
    panel_sends = []
    panel_recvs = []
    panel_passes = []
    passed_recvs = []
    front_sends = []
    front_recvs = []
    for offset in range(1, rows):
        to = row_peer(offset)
        origin = lax.rem(row + rows - offset, rows)
        for slot, group in ((row, panel_sends), (origin, panel_recvs)):
            group.append(
                pltpu.make_async_remote_copy(
                    src_ref=own_panel.at[:, source_rows],
                    dst_ref=far_panel.at[:, slot, held],
                    send_sem=panel_ssem.at[offset - 1],
                    recv_sem=panel_rsem.at[offset - 1],
                    device_id={"row": to},
                    device_id_type=MESH,
                )
            )
        for hop in range(1, shares):
            giver = lax.rem(pole + shares - hop, shares)
            theirs = pl.ds(pl.multiple_of(giver * height, height), height)
            for rows_of, group in ((held, panel_passes), (theirs, passed_recvs)):
                group.append(
                    pltpu.make_async_remote_copy(
                        src_ref=far_panel.at[:, origin, held],
                        dst_ref=far_panel.at[:, origin, rows_of],
                        send_sem=pass_ssem.at[offset - 1, hop - 1],
                        recv_sem=pass_rsem.at[offset - 1, hop - 1],
                        device_id={"pole": lax.rem(pole + hop, shares)},
                        device_id_type=MESH,
                    )
                )
        theirs = pl.ds(pl.multiple_of(to * block, block), block)
        for slot, group in ((row, front_sends), (origin, front_recvs)):
            group.append(
                pltpu.make_async_remote_copy(
                    src_ref=own_front.at[:, :, theirs],
                    dst_ref=far_front.at[:, slot],
                    send_sem=front_ssem.at[offset - 1],
                    recv_sem=front_rsem.at[offset - 1],
                    device_id={"row": to},
                    device_id_type=MESH,
                )
            )
    for copy in panel_sends:
        copy.start()

    for copy in local[2:5]:
        copy.wait()
    shift_real = shift[0, 0]
    shift_imag = shift[0, 1]

    def pass_on():
        for copy in panel_recvs:
            copy.wait_recv()
        for copy in panel_passes:
            copy.start()
        for copy in panel_sends:
            copy.wait_send()
        for copy in local[5:7]:
            copy.wait()
        for copy in front_sends:
            copy.start()

    inverse = pivot_inverse(piv_v[0], piv_v[1], shift_real, shift_imag, pass_on)
    inv_high, inv_low = split(inverse)
    inv_below = jnp.concatenate([below(inv_high), below(inv_low)], axis=0)
    for copy in local[7:]:
        copy.wait()
    weight_real = weight[0, 0]
    weight_imag = weight[0, 1]
    coupling = couple(own_panel[0], own_panel[1], shift_real, shift_imag)
    coupled = side(coupling)
    own_solved = rounded(halves(nn(side((coupled, coupled)), inv_below)))
    anc = (
        anc_v[0].reshape(rows * width, block),
        anc_v[1].reshape(rows * width, block),
    )
    swept = product(anc, own_solved)
    swept_imag = (weight_real * swept[1] + weight_imag * swept[0]).astype(BF16)
    swept_real = (weight_real * swept[0] - weight_imag * swept[1]).astype(BF16)
    swept_both = side((swept_imag.T, swept_real.T))
    own_share = (weight_real * inverse[1] + weight_imag * inverse[0]) * (1.0 / (rows * cols))
    far_panel[:, row] = own_panel[:, here]

    for copy in passed_recvs:
        copy.wait_recv()
    far_coupling = side(
        couple(
            far_panel[0].reshape(rows * width, size),
            far_panel[1].reshape(rows * width, size),
            shift_real,
            shift_imag,
        )
    )
    solved = rounded(halves(nn(jnp.concatenate([far_coupling, far_coupling], axis=1), inv_below)))

    def scatter(value, kept, sent, height):
        for index in range(layer):
            tile = value[
                (index % cols) * height : (index % cols + 1) * height,
                (index // cols) * piece : (index // cols + 1) * piece,
            ]
            kept[index] = tile
            sent[index] = tile.astype(BF16)

    def exchange(sent, received, ssem, rsem):
        copies = []
        for offset in range(1, layer):
            index, device = layer_peer(offset)
            copies.append(
                pltpu.make_async_remote_copy(
                    src_ref=sent.at[index],
                    dst_ref=received.at[offset - 1],
                    send_sem=ssem.at[offset - 1],
                    recv_sem=rsem.at[offset - 1],
                    device_id=device,
                    device_id_type=MESH,
                )
            )
        for copy in copies:
            copy.start()
        return copies

    share = own_share + nn(swept_both, jnp.concatenate(solved, axis=0))
    scatter(share, part_piv, send_piv, strip)
    piv_copies = exchange(send_piv, recv_piv, piv_ssem, piv_rsem)
    part = halves(nn(side((anc[0].T, anc[1].T)), below(solved)))
    weighted_imag = -(weight_real * part[1] + weight_imag * part[0])


    for copy in piv_copies:
        copy.wait_recv()
    layer_sum = part_piv[me]
    for offset in range(layer - 1):
        layer_sum = layer_sum + recv_piv[offset].astype(F32)
    layer_send[...] = layer_sum.astype(BF16)
    layer_copies = [
        pltpu.make_async_remote_copy(
            src_ref=layer_send,
            dst_ref=layer_recv.at[offset - 1],
            send_sem=layer_ssem.at[offset - 1],
            recv_sem=layer_rsem.at[offset - 1],
            device_id={"row": row_peer(offset)},
            device_id_type=MESH,
        )
        for offset in range(1, rows)
    ]
    for copy in layer_copies:
        copy.start()
    scatter(weighted_imag, part_rows, send_rows, width)
    rows_copies = exchange(send_rows, recv_rows, rows_ssem, rows_rsem)
    update = halves(nt(side(solved), across(coupling)))
    far_front[:, row] = own_front[:, :, mine]

    for copy in layer_copies:
        copy.wait_recv()
    whole = layer_sum
    for offset in range(rows - 1):
        whole = whole + layer_recv[offset].astype(F32)
    final_piv[...] = whole
    own_copy = pltpu.make_async_copy(final_piv, pivot_out.at[col], out_sem.at[2])
    own_copy.start()
    last_copies = []
    last_recvs = []
    for offset in range(1, cols):
        to = lax.rem(col + offset, cols)
        origin = lax.rem(col + cols - offset, cols)
        for slot, group in ((col, last_copies), (origin, last_recvs)):
            group.append(
                pltpu.make_async_remote_copy(
                    src_ref=final_piv,
                    dst_ref=pivot_out.at[slot],
                    send_sem=last_ssem.at[offset - 1],
                    recv_sem=last_rsem.at[offset - 1],
                    device_id={"col": to},
                    device_id_type=MESH,
                )
            )
    for copy in last_copies:
        copy.start()

    for copy in front_recvs:
        copy.wait_recv()
    for index in range(rows):
        flag = pattern[index, row].astype(F32)
        margin = far_front[1, index].astype(F32)
        hamil = far_front[0, index].astype(F32)
        at = slice(index * width, (index + 1) * width)
        schur_v[0, index] = (flag * (hamil - shift_real * margin) - update[0][at]).astype(BF16)
        schur_v[1, index] = (flag * (-shift_imag * margin) - update[1][at]).astype(BF16)

    schur_copy = pltpu.make_async_copy(schur_v, schur_out, out_sem.at[0])
    schur_copy.start()

    for copy in rows_copies:
        copy.wait_recv()
    rows_sum = part_rows[me]
    for offset in range(layer - 1):
        rows_sum = rows_sum + recv_rows[offset].astype(F32)
    final_rows[...] = rows_sum
    rows_copy = pltpu.make_async_copy(final_rows, rows_out, out_sem.at[1])
    rows_copy.start()

    for copy in panel_passes + front_sends + piv_copies + layer_copies + rows_copies:
        copy.wait_send()
    schur_copy.wait()
    rows_copy.wait()
    own_copy.wait()
    for copy in last_copies:
        copy.wait_send()
    for copy in last_recvs:
        copy.wait_recv()


def hand_over(*refs):
    sources, targets, staged, sems = refs[:3], refs[3:6], refs[6:9], refs[9]
    half = sources[0].shape[1] // 2
    pieces = [
        (0, (part, pl.ds(start * half, half))) for part in range(2) for start in range(2)
    ] + [(2, ()), (1, ())]
    inward = []
    outward = []
    for index, (which, at) in enumerate(pieces):
        source, stage, target = sources[which], staged[which], targets[which]
        if at:
            source, stage, target = source.at[at], stage.at[at], target.at[at]
        inward.append(pltpu.make_async_copy(source, stage, sems.at[0, index]))
        outward.append(pltpu.make_async_copy(stage, target, sems.at[1, index]))
        inward[index].start()
    for index in range(len(pieces)):
        inward[index].wait()
        outward[index].start()
    for copy in outward:
        copy.wait()


def shards(
    rows,
    cols,
    poles,
    front_h,
    front_s,
    panel_h,
    panel_s,
    pivot_h,
    pivot_s,
    pole_shift,
    pole_weight,
    pattern,
    ancestor_inverse,
):
    width = front_h.shape[0]
    block = panel_h.shape[0]
    size = pivot_h.shape[0]
    piece = size // poles
    strip = size // cols
    layer = poles * cols
    ancestor = ancestor_inverse.reshape(2, rows, width, block)
    hbm = pl.BlockSpec(memory_space=pl.ANY)
    dma = pltpu.SemaphoreType.DMA
    out_shape = (
        jax.ShapeDtypeStruct((2, rows, width, block), BF16),
        jax.ShapeDtypeStruct((width, piece), F32),
        jax.ShapeDtypeStruct((cols, strip, piece), F32),
    )
    found = pl.pallas_call(
        functools.partial(step, rows, cols, poles),
        out_shape=out_shape,
        in_specs=[hbm] * 10,
        out_specs=(hbm,) * 3,
        scratch_shapes=[
            pltpu.SMEM(pole_shift.shape, F32),
            pltpu.SMEM(pole_weight.shape, F32),
            pltpu.SMEM(pattern.shape, jnp.int32),
            pltpu.VMEM((2, size, size), BF16),
            pltpu.VMEM((2, block, size), BF16),
            pltpu.VMEM((2,) + front_h.shape, BF16),
            pltpu.VMEM((2, rows, width, size), BF16),
            pltpu.VMEM((2, rows, width, block), BF16),
            pltpu.VMEM((2, rows, width, block), BF16),
            pltpu.VMEM((2, rows, width, block), BF16),
            pltpu.VMEM((width, piece), F32),
            pltpu.VMEM((strip, piece), F32),
            pltpu.VMEM((layer, width, piece), F32),
            pltpu.VMEM((layer, strip, piece), F32),
            pltpu.VMEM((layer, width, piece), BF16),
            pltpu.VMEM((layer, strip, piece), BF16),
            pltpu.VMEM((layer - 1, width, piece), BF16),
            pltpu.VMEM((layer - 1, strip, piece), BF16),
            pltpu.VMEM((strip, piece), BF16),
            pltpu.VMEM((rows - 1, strip, piece), BF16),
            dma((rows - 1, poles - 1)),
            dma((rows - 1, poles - 1)),
            dma((10,)),
            dma((rows - 1,)),
            dma((rows - 1,)),
            dma((rows - 1,)),
            dma((rows - 1,)),
            dma((layer - 1,)),
            dma((layer - 1,)),
            dma((layer - 1,)),
            dma((layer - 1,)),
            dma((rows - 1,)),
            dma((rows - 1,)),
            dma((cols - 1,)),
            dma((cols - 1,)),
            dma((3,)),
        ],
        compiler_params=pltpu.CompilerParams(
            collective_id=0, has_side_effects=True, vmem_limit_bytes=60 * 1024 * 1024
        ),
        name="front_step",
    )(
        pole_shift,
        pole_weight,
        pattern,
        front_h,
        front_s,
        panel_h,
        panel_s,
        pivot_h,
        pivot_s,
        ancestor,
    )
    schur, rows_out, pivot_out = pl.pallas_call(
        hand_over,
        out_shape=out_shape,
        in_specs=[hbm] * 3,
        out_specs=(hbm,) * 3,
        scratch_shapes=[pltpu.VMEM(part.shape, part.dtype) for part in out_shape]
        + [dma((2, 6))],
        compiler_params=pltpu.CompilerParams(vmem_limit_bytes=60 * 1024 * 1024),
        name="hand_over",
    )(*found)
    return (
        schur.reshape(ancestor_inverse.shape),
        rows_out,
        pivot_out.reshape(size, piece),
    )


def solution(mesh):
    sizes = dict(mesh.shape)
    in_specs = (
        P(("row", "col"), None),
        P(("row", "col"), None),
        P("row", None),
        P("row", None),
        P(),
        P(),
        P("pole", None),
        P("pole", None),
        P(),
        P("pole", None, None, "col", None, "row"),
    )
    out_specs = (
        P("pole", None, None, "col", None, "row"),
        P(("row", "col"), "pole"),
        P(None, "pole"),
    )
    body = functools.partial(shards, sizes["row"], sizes["col"], sizes["pole"])
    return jax.shard_map(body, mesh=mesh, in_specs=in_specs, out_specs=out_specs, check_vma=False)
```

```python
import functools

import jax
import jax.numpy as jnp
from jax import lax
from jax.experimental import pallas as pl
from jax.experimental.pallas import tpu as pltpu
from jax.sharding import PartitionSpec as P

MESH = pl.DeviceIdType.MESH
F32 = jnp.float32
BF16 = jnp.bfloat16


def nn(left, right):
    return lax.dot_general(left, right, (((1,), (0,)), ((), ())), preferred_element_type=F32)


def nt(left, right):
    return lax.dot_general(left, right, (((1,), (1,)), ((), ())), preferred_element_type=F32)


def side(pair):
    return jnp.concatenate(pair, axis=1)


def below(pair):
    real, imag = pair
    return jnp.concatenate([side((real, imag)), side((-imag, real))], axis=0)


def across(pair):
    real, imag = pair
    return jnp.concatenate([side((real, -imag)), side((imag, real))], axis=0)


def halves(value):
    middle = value.shape[1] // 2
    return value[:, :middle], value[:, middle:]


def product(left, right):
    return halves(nn(side(left), below(right)))


def rounded(pair):
    return pair[0].astype(BF16), pair[1].astype(BF16)


def split(pair):
    high = rounded(pair)
    low = rounded((pair[0] - high[0].astype(F32), pair[1] - high[1].astype(F32)))
    return high, low


def plus(left, right):
    return left[0] + right[0], left[1] + right[1]


def couple(rows_h, rows_s, shift_real, shift_imag):
    margin = rows_s.astype(F32)
    real = rows_h.astype(F32) - shift_real * margin
    return real.astype(BF16), (-shift_imag * margin).astype(BF16)


def pivot_inverse(pivot_h, pivot_s, shift_real, shift_imag, meanwhile):
    size = pivot_h.shape[0]
    margin = pivot_s.astype(F32)
    real = pivot_h.astype(F32) - shift_real * margin
    imag = -shift_imag * margin
    on_diagonal = lax.broadcasted_iota(jnp.int32, (size, size), 0) == lax.broadcasted_iota(
        jnp.int32, (size, size), 1
    )
    only_real = jnp.where(on_diagonal, real, 0.0)
    only_imag = jnp.where(on_diagonal, imag, 0.0)

    def start(axis):
        diag_real = jnp.sum(only_real, axis=axis, keepdims=True)
        diag_imag = jnp.sum(only_imag, axis=axis, keepdims=True)
        denom = diag_real * diag_real + diag_imag * diag_imag
        return diag_real / denom, -diag_imag / denom

    left_real, left_imag = start(1)
    right_real, right_imag = start(0)
    identity = jnp.where(on_diagonal, 1.0, 0.0)
    first = (
        identity - (left_real * real - left_imag * imag),
        -(left_real * imag + left_imag * real),
    )
    first_b = rounded(first)
    second = product(first_b, first_b)
    second_b = rounded(second)
    tall = nn(jnp.concatenate([side(first_b), side(second_b)], axis=0), below(second_b))
    third = halves(tall[:size])
    fourth_b = rounded(halves(tall[size:]))
    total = plus(plus((identity + first[0], first[1]), second), third)
    tall = nn(
        jnp.concatenate([side(fourth_b), side(rounded(total))], axis=0), below(fourth_b)
    )
    eighth_b = rounded(halves(tall[:size]))
    total = plus(total, halves(tall[size:]))
    meanwhile()
    total = plus(total, product(rounded(total), eighth_b))
    return (
        total[0] * right_real - total[1] * right_imag,
        total[0] * right_imag + total[1] * right_real,
    )


def step(
    rows,
    cols,
    poles,
    shift_hbm,
    weight_hbm,
    pattern_hbm,
    front_h,
    front_s,
    panel_h,
    panel_s,
    pivot_h,
    pivot_s,
    ancestor,
    schur_out,
    rows_out,
    pivot_out,
    shift,
    weight,
    pattern,
    piv_v,
    own_panel,
    own_front,
    far_panel,
    far_front,
    anc_v,
    schur_v,
    final_rows,
    final_piv,
    part_rows,
    part_piv,
    send_rows,
    send_piv,
    recv_rows,
    recv_piv,
    layer_send,
    layer_recv,
    pass_ssem,
    pass_rsem,
    local_sem,
    panel_ssem,
    panel_rsem,
    front_ssem,
    front_rsem,
    rows_ssem,
    rows_rsem,
    piv_ssem,
    piv_rsem,
    layer_ssem,
    layer_rsem,
    last_ssem,
    last_rsem,
    out_sem,
):
    row = lax.axis_index("row")
    col = lax.axis_index("col")
    pole = lax.axis_index("pole")
    layer = poles * cols
    me = pole * cols + col
    width = front_h.shape[0]
    block = panel_h.shape[0]
    size = pivot_h.shape[0]
    piece = size // poles
    strip = size // cols

    def row_peer(offset):
        return lax.rem(row + offset, rows)

    def layer_peer(offset):
        index = lax.rem(me + offset, layer)
        return index, {"pole": index // cols, "col": lax.rem(index, cols)}

    barrier = pltpu.get_barrier_semaphore()
    for offset in range(1, rows):
        pl.semaphore_signal(
            barrier, inc=1, device_id={"row": row_peer(offset)}, device_id_type=MESH
        )
    for offset in range(1, layer):
        pl.semaphore_signal(
            barrier, inc=1, device_id=layer_peer(offset)[1], device_id_type=MESH
        )

    here = pl.ds(pl.multiple_of(col * width, width), width)
    mine = pl.ds(pl.multiple_of(row * block, block), block)
    local = [
        pltpu.make_async_copy(source, target, local_sem.at[index])
        for index, (source, target) in enumerate(
            [
                (panel_h, own_panel.at[0]),
                (panel_s, own_panel.at[1]),
                (shift_hbm, shift),
                (pivot_h, piv_v.at[0]),
                (pivot_s, piv_v.at[1]),
                (front_h, own_front.at[0]),
                (front_s, own_front.at[1]),
                (weight_hbm, weight),
                (pattern_hbm, pattern),
                (ancestor, anc_v),
            ]
        )
    ]
    for copy in local:
        copy.start()
    pl.semaphore_wait(barrier, rows - 1 + layer - 1)
    for copy in local[:2]:
        copy.wait()

    shares = 1
    height = width // shares
    first = pl.multiple_of(pole * height if shares > 1 else 0, height)
    held = pl.ds(first, height)
    source_rows = pl.ds(pl.multiple_of(col * width + first, height), height)
    panel_sends = []
    panel_recvs = []
    panel_passes = []
    passed_recvs = []
    front_sends = []
    front_recvs = []
    for offset in range(1, rows):
        to = row_peer(offset)
        origin = lax.rem(row + rows - offset, rows)
        for slot, group in ((row, panel_sends), (origin, panel_recvs)):
            group.append(
                pltpu.make_async_remote_copy(
                    src_ref=own_panel.at[:, source_rows],
                    dst_ref=far_panel.at[:, slot, held],
                    send_sem=panel_ssem.at[offset - 1],
                    recv_sem=panel_rsem.at[offset - 1],
                    device_id={"row": to},
                    device_id_type=MESH,
                )
            )
        for hop in range(1, shares):
            giver = lax.rem(pole + shares - hop, shares)
            theirs = pl.ds(pl.multiple_of(giver * height, height), height)
            for rows_of, group in ((held, panel_passes), (theirs, passed_recvs)):
                group.append(
                    pltpu.make_async_remote_copy(
                        src_ref=far_panel.at[:, origin, held],
                        dst_ref=far_panel.at[:, origin, rows_of],
                        send_sem=pass_ssem.at[offset - 1, hop - 1],
                        recv_sem=pass_rsem.at[offset - 1, hop - 1],
                        device_id={"pole": lax.rem(pole + hop, shares)},
                        device_id_type=MESH,
                    )
                )
        theirs = pl.ds(pl.multiple_of(to * block, block), block)
        for slot, group in ((row, front_sends), (origin, front_recvs)):
            group.append(
                pltpu.make_async_remote_copy(
                    src_ref=own_front.at[:, :, theirs],
                    dst_ref=far_front.at[:, slot],
                    send_sem=front_ssem.at[offset - 1],
                    recv_sem=front_rsem.at[offset - 1],
                    device_id={"row": to},
                    device_id_type=MESH,
                )
            )
    for copy in panel_sends:
        copy.start()

    for copy in local[2:5]:
        copy.wait()
    shift_real = shift[0, 0]
    shift_imag = shift[0, 1]

    def pass_on():
        for copy in panel_sends:
            copy.wait_send()
        for copy in local[5:7]:
            copy.wait()
        for copy in front_sends:
            copy.start()

    inverse = pivot_inverse(piv_v[0], piv_v[1], shift_real, shift_imag, pass_on)
    inv_high, inv_low = split(inverse)
    inv_below = jnp.concatenate([below(inv_high), below(inv_low)], axis=0)
    for copy in local[7:]:
        copy.wait()
    weight_real = weight[0, 0]
    weight_imag = weight[0, 1]
    coupling = couple(own_panel[0], own_panel[1], shift_real, shift_imag)
    coupled = side(coupling)
    own_solved = rounded(halves(nn(coupled, inv_below[: 2 * size])))
    anc = (
        anc_v[0].reshape(rows * width, block),
        anc_v[1].reshape(rows * width, block),
    )
    swept = product(anc, own_solved)
    swept_imag = (weight_real * swept[1] + weight_imag * swept[0]).astype(BF16)
    swept_real = (weight_real * swept[0] - weight_imag * swept[1]).astype(BF16)
    swept_both = side((swept_imag.T, swept_real.T))
    own_share = (weight_real * inverse[1] + weight_imag * inverse[0]) * (1.0 / (rows * cols))
    far_panel[:, row] = own_panel[:, here]

    for copy in panel_recvs:
        copy.wait_recv()
    far_coupling = side(
        couple(
            far_panel[0].reshape(rows * width, size),
            far_panel[1].reshape(rows * width, size),
            shift_real,
            shift_imag,
        )
    )
    solved = rounded(halves(nn(jnp.concatenate([far_coupling, far_coupling], axis=1), inv_below)))

    def scatter(value, kept, sent, height):
        for index in range(layer):
            tile = value[
                (index % cols) * height : (index % cols + 1) * height,
                (index // cols) * piece : (index // cols + 1) * piece,
            ]
            kept[index] = tile
            sent[index] = tile.astype(BF16)

    def exchange(sent, received, ssem, rsem):
        copies = []
        for offset in range(1, layer):
            index, device = layer_peer(offset)
            copies.append(
                pltpu.make_async_remote_copy(
                    src_ref=sent.at[index],
                    dst_ref=received.at[offset - 1],
                    send_sem=ssem.at[offset - 1],
                    recv_sem=rsem.at[offset - 1],
                    device_id=device,
                    device_id_type=MESH,
                )
            )
        for copy in copies:
            copy.start()
        return copies

    share = own_share + nn(swept_both, jnp.concatenate(solved, axis=0))
    scatter(share, part_piv, send_piv, strip)
    piv_copies = exchange(send_piv, recv_piv, piv_ssem, piv_rsem)
    part = halves(nn(side((anc[0].T, anc[1].T)), below(solved)))
    weighted_imag = -(weight_real * part[1] + weight_imag * part[0])
    scatter(weighted_imag, part_rows, send_rows, width)

    update = halves(nt(side(solved), across(coupling)))
    far_front[:, row] = own_front[:, :, mine]

    for copy in piv_copies:
        copy.wait_recv()
    layer_sum = part_piv[me]
    for offset in range(layer - 1):
        layer_sum = layer_sum + recv_piv[offset].astype(F32)
    layer_send[...] = layer_sum.astype(BF16)
    layer_copies = [
        pltpu.make_async_remote_copy(
            src_ref=layer_send,
            dst_ref=layer_recv.at[offset - 1],
            send_sem=layer_ssem.at[offset - 1],
            recv_sem=layer_rsem.at[offset - 1],
            device_id={"row": row_peer(offset)},
            device_id_type=MESH,
        )
        for offset in range(1, rows)
    ]
    for copy in layer_copies:
        copy.start()
    rows_copies = exchange(send_rows, recv_rows, rows_ssem, rows_rsem)

    for copy in layer_copies:
        copy.wait_recv()
    whole = layer_sum
    for offset in range(rows - 1):
        whole = whole + layer_recv[offset].astype(F32)
    final_piv[...] = whole
    own_copy = pltpu.make_async_copy(final_piv, pivot_out.at[col], out_sem.at[2])
    own_copy.start()
    last_copies = []
    last_recvs = []
    for offset in range(1, cols):
        to = lax.rem(col + offset, cols)
        origin = lax.rem(col + cols - offset, cols)
        for slot, group in ((col, last_copies), (origin, last_recvs)):
            group.append(
                pltpu.make_async_remote_copy(
                    src_ref=final_piv,
                    dst_ref=pivot_out.at[slot],
                    send_sem=last_ssem.at[offset - 1],
                    recv_sem=last_rsem.at[offset - 1],
                    device_id={"col": to},
                    device_id_type=MESH,
                )
            )
    for copy in last_copies:
        copy.start()

    for copy in front_recvs:
        copy.wait_recv()
    for index in range(rows):
        flag = pattern[index, row].astype(F32)
        margin = far_front[1, index].astype(F32)
        hamil = far_front[0, index].astype(F32)
        at = slice(index * width, (index + 1) * width)
        schur_v[0, index] = (flag * (hamil - shift_real * margin) - update[0][at]).astype(BF16)
        schur_v[1, index] = (flag * (-shift_imag * margin) - update[1][at]).astype(BF16)

    schur_copy = pltpu.make_async_copy(schur_v, schur_out, out_sem.at[0])
    schur_copy.start()

    for copy in rows_copies:
        copy.wait_recv()
    rows_sum = part_rows[me]
    for offset in range(layer - 1):
        rows_sum = rows_sum + recv_rows[offset].astype(F32)
    final_rows[...] = rows_sum
    rows_copy = pltpu.make_async_copy(final_rows, rows_out, out_sem.at[1])
    rows_copy.start()

    for copy in panel_passes + front_sends + piv_copies + layer_copies + rows_copies:
        copy.wait_send()
    schur_copy.wait()
    rows_copy.wait()
    own_copy.wait()
    for copy in last_copies:
        copy.wait_send()
    for copy in last_recvs:
        copy.wait_recv()


def hand_over(*refs):
    sources, targets, staged, sems = refs[:3], refs[3:6], refs[6:9], refs[9]
    inward = []
    outward = []
    for index in range(3):
        inward.append(
            pltpu.make_async_copy(sources[index], staged[index], sems.at[0, index])
        )
        outward.append(
            pltpu.make_async_copy(staged[index], targets[index], sems.at[1, index])
        )
        inward[index].start()
    for index in range(3):
        inward[index].wait()
        outward[index].start()
    for copy in outward:
        copy.wait()


def shards(
    rows,
    cols,
    poles,
    front_h,
    front_s,
    panel_h,
    panel_s,
    pivot_h,
    pivot_s,
    pole_shift,
    pole_weight,
    pattern,
    ancestor_inverse,
):
    width = front_h.shape[0]
    block = panel_h.shape[0]
    size = pivot_h.shape[0]
    piece = size // poles
    strip = size // cols
    layer = poles * cols
    ancestor = ancestor_inverse.reshape(2, rows, width, block)
    hbm = pl.BlockSpec(memory_space=pl.ANY)
    dma = pltpu.SemaphoreType.DMA
    out_shape = (
        jax.ShapeDtypeStruct((2, rows, width, block), BF16),
        jax.ShapeDtypeStruct((width, piece), F32),
        jax.ShapeDtypeStruct((cols, strip, piece), F32),
    )
    found = pl.pallas_call(
        functools.partial(step, rows, cols, poles),
        out_shape=out_shape,
        in_specs=[hbm] * 10,
        out_specs=(hbm,) * 3,
        scratch_shapes=[
            pltpu.SMEM(pole_shift.shape, F32),
            pltpu.SMEM(pole_weight.shape, F32),
            pltpu.SMEM(pattern.shape, jnp.int32),
            pltpu.VMEM((2, size, size), BF16),
            pltpu.VMEM((2, block, size), BF16),
            pltpu.VMEM((2,) + front_h.shape, BF16),
            pltpu.VMEM((2, rows, width, size), BF16),
            pltpu.VMEM((2, rows, width, block), BF16),
            pltpu.VMEM((2, rows, width, block), BF16),
            pltpu.VMEM((2, rows, width, block), BF16),
            pltpu.VMEM((width, piece), F32),
            pltpu.VMEM((strip, piece), F32),
            pltpu.VMEM((layer, width, piece), F32),
            pltpu.VMEM((layer, strip, piece), F32),
            pltpu.VMEM((layer, width, piece), BF16),
            pltpu.VMEM((layer, strip, piece), BF16),
            pltpu.VMEM((layer - 1, width, piece), BF16),
            pltpu.VMEM((layer - 1, strip, piece), BF16),
            pltpu.VMEM((strip, piece), BF16),
            pltpu.VMEM((rows - 1, strip, piece), BF16),
            dma((rows - 1, poles - 1)),
            dma((rows - 1, poles - 1)),
            dma((10,)),
            dma((rows - 1,)),
            dma((rows - 1,)),
            dma((rows - 1,)),
            dma((rows - 1,)),
            dma((layer - 1,)),
            dma((layer - 1,)),
            dma((layer - 1,)),
            dma((layer - 1,)),
            dma((rows - 1,)),
            dma((rows - 1,)),
            dma((cols - 1,)),
            dma((cols - 1,)),
            dma((3,)),
        ],
        compiler_params=pltpu.CompilerParams(
            collective_id=0, has_side_effects=True, vmem_limit_bytes=60 * 1024 * 1024
        ),
        name="front_step",
    )(
        pole_shift,
        pole_weight,
        pattern,
        front_h,
        front_s,
        panel_h,
        panel_s,
        pivot_h,
        pivot_s,
        ancestor,
    )
    schur, rows_out, pivot_out = pl.pallas_call(
        hand_over,
        out_shape=out_shape,
        in_specs=[hbm] * 3,
        out_specs=(hbm,) * 3,
        scratch_shapes=[pltpu.VMEM(part.shape, part.dtype) for part in out_shape]
        + [dma((2, 3))],
        compiler_params=pltpu.CompilerParams(vmem_limit_bytes=60 * 1024 * 1024),
        name="hand_over",
    )(*found)
    return (
        schur.reshape(ancestor_inverse.shape),
        rows_out,
        pivot_out.reshape(size, piece),
    )


def solution(mesh):
    sizes = dict(mesh.shape)
    in_specs = (
        P(("row", "col"), None),
        P(("row", "col"), None),
        P("row", None),
        P("row", None),
        P(),
        P(),
        P("pole", None),
        P("pole", None),
        P(),
        P("pole", None, None, "col", None, "row"),
    )
    out_specs = (
        P("pole", None, None, "col", None, "row"),
        P(("row", "col"), "pole"),
        P(None, "pole"),
    )
    body = functools.partial(shards, sizes["row"], sizes["col"], sizes["pole"])
    return jax.shard_map(body, mesh=mesh, in_specs=in_specs, out_specs=out_specs, check_vma=False)
```

```python
import functools

import jax
import jax.numpy as jnp
from jax import lax
from jax.experimental import pallas as pl
from jax.experimental.pallas import tpu as pltpu
from jax.sharding import PartitionSpec as P

MESH = pl.DeviceIdType.MESH
F32 = jnp.float32
BF16 = jnp.bfloat16


def nn(left, right):
    return lax.dot_general(left, right, (((1,), (0,)), ((), ())), preferred_element_type=F32)


def nt(left, right):
    return lax.dot_general(left, right, (((1,), (1,)), ((), ())), preferred_element_type=F32)


def side(pair):
    return jnp.concatenate(pair, axis=1)


def below(pair):
    real, imag = pair
    return jnp.concatenate([side((real, imag)), side((-imag, real))], axis=0)


def across(pair):
    real, imag = pair
    return jnp.concatenate([side((real, -imag)), side((imag, real))], axis=0)


def halves(value):
    middle = value.shape[1] // 2
    return value[:, :middle], value[:, middle:]


def product(left, right):
    return halves(nn(side(left), below(right)))


def rounded(pair):
    return pair[0].astype(BF16), pair[1].astype(BF16)


def split(pair):
    high = rounded(pair)
    low = rounded((pair[0] - high[0].astype(F32), pair[1] - high[1].astype(F32)))
    return high, low


def plus(left, right):
    return left[0] + right[0], left[1] + right[1]


def couple(rows_h, rows_s, shift_real, shift_imag):
    margin = rows_s.astype(F32)
    real = rows_h.astype(F32) - shift_real * margin
    return real.astype(BF16), (-shift_imag * margin).astype(BF16)


def pivot_inverse(pivot_h, pivot_s, shift_real, shift_imag, meanwhile):
    size = pivot_h.shape[0]
    margin = pivot_s.astype(F32)
    real = pivot_h.astype(F32) - shift_real * margin
    imag = -shift_imag * margin
    on_diagonal = lax.broadcasted_iota(jnp.int32, (size, size), 0) == lax.broadcasted_iota(
        jnp.int32, (size, size), 1
    )
    only_real = jnp.where(on_diagonal, real, 0.0)
    only_imag = jnp.where(on_diagonal, imag, 0.0)

    def start(axis):
        diag_real = jnp.sum(only_real, axis=axis, keepdims=True)
        diag_imag = jnp.sum(only_imag, axis=axis, keepdims=True)
        denom = diag_real * diag_real + diag_imag * diag_imag
        return diag_real / denom, -diag_imag / denom

    left_real, left_imag = start(1)
    right_real, right_imag = start(0)
    identity = jnp.where(on_diagonal, 1.0, 0.0)
    first = (
        identity - (left_real * real - left_imag * imag),
        -(left_real * imag + left_imag * real),
    )
    first_b = rounded(first)
    second = product(first_b, first_b)
    second_b = rounded(second)
    tall = nn(jnp.concatenate([side(first_b), side(second_b)], axis=0), below(second_b))
    third = halves(tall[:size])
    fourth_b = rounded(halves(tall[size:]))
    total = plus(plus((identity + first[0], first[1]), second), third)
    tall = nn(
        jnp.concatenate([side(fourth_b), side(rounded(total))], axis=0), below(fourth_b)
    )
    eighth_b = rounded(halves(tall[:size]))
    total = plus(total, halves(tall[size:]))
    meanwhile()
    total = plus(total, product(rounded(total), eighth_b))
    return (
        total[0] * right_real - total[1] * right_imag,
        total[0] * right_imag + total[1] * right_real,
    )


def step(
    rows,
    cols,
    poles,
    shift_hbm,
    weight_hbm,
    pattern_hbm,
    front_h,
    front_s,
    panel_h,
    panel_s,
    pivot_h,
    pivot_s,
    ancestor,
    schur_out,
    rows_out,
    pivot_out,
    shift,
    weight,
    pattern,
    piv_v,
    own_panel,
    own_front,
    far_panel,
    far_front,
    anc_v,
    schur_v,
    final_rows,
    final_piv,
    part_rows,
    part_piv,
    send_rows,
    send_piv,
    recv_rows,
    recv_piv,
    layer_send,
    layer_recv,
    pass_ssem,
    pass_rsem,
    local_sem,
    panel_ssem,
    panel_rsem,
    front_ssem,
    front_rsem,
    rows_ssem,
    rows_rsem,
    piv_ssem,
    piv_rsem,
    layer_ssem,
    layer_rsem,
    last_ssem,
    last_rsem,
    out_sem,
):
    row = lax.axis_index("row")
    col = lax.axis_index("col")
    pole = lax.axis_index("pole")
    layer = poles * cols
    me = pole * cols + col
    width = front_h.shape[0]
    block = panel_h.shape[0]
    size = pivot_h.shape[0]
    piece = size // poles
    strip = size // cols

    def row_peer(offset):
        return lax.rem(row + offset, rows)

    def layer_peer(offset):
        index = lax.rem(me + offset, layer)
        return index, {"pole": index // cols, "col": lax.rem(index, cols)}

    barrier = pltpu.get_barrier_semaphore()
    for offset in range(1, rows):
        pl.semaphore_signal(
            barrier, inc=1, device_id={"row": row_peer(offset)}, device_id_type=MESH
        )
    for offset in range(1, layer):
        pl.semaphore_signal(
            barrier, inc=1, device_id=layer_peer(offset)[1], device_id_type=MESH
        )

    here = pl.ds(pl.multiple_of(col * width, width), width)
    mine = pl.ds(pl.multiple_of(row * block, block), block)
    local = [
        pltpu.make_async_copy(source, target, local_sem.at[index])
        for index, (source, target) in enumerate(
            [
                (panel_h, own_panel.at[0]),
                (panel_s, own_panel.at[1]),
                (shift_hbm, shift),
                (pivot_h, piv_v.at[0]),
                (pivot_s, piv_v.at[1]),
                (front_h, own_front.at[0]),
                (front_s, own_front.at[1]),
                (weight_hbm, weight),
                (pattern_hbm, pattern),
                (ancestor, anc_v),
            ]
        )
    ]
    for copy in local:
        copy.start()
    pl.semaphore_wait(barrier, rows - 1 + layer - 1)
    for copy in local[:2]:
        copy.wait()

    shares = poles if width % (16 * poles) == 0 else 1
    height = width // shares
    first = pl.multiple_of(pole * height if shares > 1 else 0, height)
    held = pl.ds(first, height)
    source_rows = pl.ds(pl.multiple_of(col * width + first, height), height)
    panel_sends = []
    panel_recvs = []
    panel_passes = []
    passed_recvs = []
    front_sends = []
    front_recvs = []
    for offset in range(1, rows):
        to = row_peer(offset)
        origin = lax.rem(row + rows - offset, rows)
        for slot, group in ((row, panel_sends), (origin, panel_recvs)):
            group.append(
                pltpu.make_async_remote_copy(
                    src_ref=own_panel.at[:, source_rows],
                    dst_ref=far_panel.at[:, slot, held],
                    send_sem=panel_ssem.at[offset - 1],
                    recv_sem=panel_rsem.at[offset - 1],
                    device_id={"row": to},
                    device_id_type=MESH,
                )
            )
        for hop in range(1, shares):
            giver = lax.rem(pole + shares - hop, shares)
            theirs = pl.ds(pl.multiple_of(giver * height, height), height)
            for rows_of, group in ((held, panel_passes), (theirs, passed_recvs)):
                group.append(
                    pltpu.make_async_remote_copy(
                        src_ref=far_panel.at[:, origin, held],
                        dst_ref=far_panel.at[:, origin, rows_of],
                        send_sem=pass_ssem.at[offset - 1, hop - 1],
                        recv_sem=pass_rsem.at[offset - 1, hop - 1],
                        device_id={"pole": lax.rem(pole + hop, shares)},
                        device_id_type=MESH,
                    )
                )
        theirs = pl.ds(pl.multiple_of(to * block, block), block)
        for slot, group in ((row, front_sends), (origin, front_recvs)):
            group.append(
                pltpu.make_async_remote_copy(
                    src_ref=own_front.at[:, :, theirs],
                    dst_ref=far_front.at[:, slot],
                    send_sem=front_ssem.at[offset - 1],
                    recv_sem=front_rsem.at[offset - 1],
                    device_id={"row": to},
                    device_id_type=MESH,
                )
            )
    for copy in panel_sends:
        copy.start()

    for copy in local[2:5]:
        copy.wait()
    shift_real = shift[0, 0]
    shift_imag = shift[0, 1]

    def pass_on():
        for index, copy in enumerate(panel_recvs):
            copy.wait_recv()
            for passed in panel_passes[index * (shares - 1) : (index + 1) * (shares - 1)]:
                passed.start()
        for copy in panel_sends:
            copy.wait_send()
        for copy in local[5:7]:
            copy.wait()
        for copy in front_sends:
            copy.start()

    inverse = pivot_inverse(piv_v[0], piv_v[1], shift_real, shift_imag, pass_on)
    inv_high, inv_low = split(inverse)
    inv_below = jnp.concatenate([below(inv_high), below(inv_low)], axis=0)
    for copy in local[7:]:
        copy.wait()
    weight_real = weight[0, 0]
    weight_imag = weight[0, 1]
    coupling = couple(own_panel[0], own_panel[1], shift_real, shift_imag)
    coupled = side(coupling)
    own_solved = rounded(halves(nn(side((coupled, coupled)), inv_below)))
    anc = (
        anc_v[0].reshape(rows * width, block),
        anc_v[1].reshape(rows * width, block),
    )
    swept = product(anc, own_solved)
    swept_imag = (weight_real * swept[1] + weight_imag * swept[0]).astype(BF16)
    swept_real = (weight_real * swept[0] - weight_imag * swept[1]).astype(BF16)
    swept_both = side((swept_imag.T, swept_real.T))
    own_share = (weight_real * inverse[1] + weight_imag * inverse[0]) * (1.0 / (rows * cols))
    far_panel[:, row] = own_panel[:, here]

    for copy in passed_recvs:
        copy.wait_recv()
    far_coupling = side(
        couple(
            far_panel[0].reshape(rows * width, size),
            far_panel[1].reshape(rows * width, size),
            shift_real,
            shift_imag,
        )
    )
    solved = rounded(halves(nn(jnp.concatenate([far_coupling, far_coupling], axis=1), inv_below)))

    def scatter(value, kept, sent, height):
        for index in range(layer):
            tile = value[
                (index % cols) * height : (index % cols + 1) * height,
                (index // cols) * piece : (index // cols + 1) * piece,
            ]
            kept[index] = tile
            sent[index] = tile.astype(BF16)

    def exchange(sent, received, ssem, rsem):
        copies = []
        for offset in range(1, layer):
            index, device = layer_peer(offset)
            copies.append(
                pltpu.make_async_remote_copy(
                    src_ref=sent.at[index],
                    dst_ref=received.at[offset - 1],
                    send_sem=ssem.at[offset - 1],
                    recv_sem=rsem.at[offset - 1],
                    device_id=device,
                    device_id_type=MESH,
                )
            )
        for copy in copies:
            copy.start()
        return copies

    share = own_share + nn(swept_both, jnp.concatenate(solved, axis=0))
    scatter(share, part_piv, send_piv, strip)
    piv_copies = exchange(send_piv, recv_piv, piv_ssem, piv_rsem)
    part = halves(nn(side((anc[0].T, anc[1].T)), below(solved)))
    weighted_imag = -(weight_real * part[1] + weight_imag * part[0])
    scatter(weighted_imag, part_rows, send_rows, width)

    update = halves(nt(side(solved), across(coupling)))
    far_front[:, row] = own_front[:, :, mine]

    for copy in piv_copies:
        copy.wait_recv()
    layer_sum = part_piv[me]
    for offset in range(layer - 1):
        layer_sum = layer_sum + recv_piv[offset].astype(F32)
    layer_send[...] = layer_sum.astype(BF16)
    layer_copies = [
        pltpu.make_async_remote_copy(
            src_ref=layer_send,
            dst_ref=layer_recv.at[offset - 1],
            send_sem=layer_ssem.at[offset - 1],
            recv_sem=layer_rsem.at[offset - 1],
            device_id={"row": row_peer(offset)},
            device_id_type=MESH,
        )
        for offset in range(1, rows)
    ]
    for copy in layer_copies:
        copy.start()
    rows_copies = exchange(send_rows, recv_rows, rows_ssem, rows_rsem)

    for copy in layer_copies:
        copy.wait_recv()
    whole = layer_sum
    for offset in range(rows - 1):
        whole = whole + layer_recv[offset].astype(F32)
    final_piv[...] = whole
    own_copy = pltpu.make_async_copy(final_piv, pivot_out.at[col], out_sem.at[2])
    own_copy.start()
    last_copies = []
    last_recvs = []
    for offset in range(1, cols):
        to = lax.rem(col + offset, cols)
        origin = lax.rem(col + cols - offset, cols)
        for slot, group in ((col, last_copies), (origin, last_recvs)):
            group.append(
                pltpu.make_async_remote_copy(
                    src_ref=final_piv,
                    dst_ref=pivot_out.at[slot],
                    send_sem=last_ssem.at[offset - 1],
                    recv_sem=last_rsem.at[offset - 1],
                    device_id={"col": to},
                    device_id_type=MESH,
                )
            )
    for copy in last_copies:
        copy.start()

    for copy in front_recvs:
        copy.wait_recv()
    for index in range(rows):
        flag = pattern[index, row].astype(F32)
        margin = far_front[1, index].astype(F32)
        hamil = far_front[0, index].astype(F32)
        at = slice(index * width, (index + 1) * width)
        schur_v[0, index] = (flag * (hamil - shift_real * margin) - update[0][at]).astype(BF16)
        schur_v[1, index] = (flag * (-shift_imag * margin) - update[1][at]).astype(BF16)

    schur_copy = pltpu.make_async_copy(schur_v, schur_out, out_sem.at[0])
    schur_copy.start()

    for copy in rows_copies:
        copy.wait_recv()
    rows_sum = part_rows[me]
    for offset in range(layer - 1):
        rows_sum = rows_sum + recv_rows[offset].astype(F32)
    final_rows[...] = rows_sum
    rows_copy = pltpu.make_async_copy(final_rows, rows_out, out_sem.at[1])
    rows_copy.start()

    for copy in panel_passes + front_sends + piv_copies + layer_copies + rows_copies:
        copy.wait_send()
    schur_copy.wait()
    rows_copy.wait()
    own_copy.wait()
    for copy in last_copies:
        copy.wait_send()
    for copy in last_recvs:
        copy.wait_recv()


def hand_over(*refs):
    sources, targets, staged, sems = refs[:3], refs[3:6], refs[6:9], refs[9]
    inward = []
    outward = []
    for index in range(3):
        inward.append(
            pltpu.make_async_copy(sources[index], staged[index], sems.at[0, index])
        )
        outward.append(
            pltpu.make_async_copy(staged[index], targets[index], sems.at[1, index])
        )
        inward[index].start()
    for index in range(3):
        inward[index].wait()
        outward[index].start()
    for copy in outward:
        copy.wait()


def shards(
    rows,
    cols,
    poles,
    front_h,
    front_s,
    panel_h,
    panel_s,
    pivot_h,
    pivot_s,
    pole_shift,
    pole_weight,
    pattern,
    ancestor_inverse,
):
    width = front_h.shape[0]
    block = panel_h.shape[0]
    size = pivot_h.shape[0]
    piece = size // poles
    strip = size // cols
    layer = poles * cols
    ancestor = ancestor_inverse.reshape(2, rows, width, block)
    hbm = pl.BlockSpec(memory_space=pl.ANY)
    dma = pltpu.SemaphoreType.DMA
    out_shape = (
        jax.ShapeDtypeStruct((2, rows, width, block), BF16),
        jax.ShapeDtypeStruct((width, piece), F32),
        jax.ShapeDtypeStruct((cols, strip, piece), F32),
    )
    found = pl.pallas_call(
        functools.partial(step, rows, cols, poles),
        out_shape=out_shape,
        in_specs=[hbm] * 10,
        out_specs=(hbm,) * 3,
        scratch_shapes=[
            pltpu.SMEM(pole_shift.shape, F32),
            pltpu.SMEM(pole_weight.shape, F32),
            pltpu.SMEM(pattern.shape, jnp.int32),
            pltpu.VMEM((2, size, size), BF16),
            pltpu.VMEM((2, block, size), BF16),
            pltpu.VMEM((2,) + front_h.shape, BF16),
            pltpu.VMEM((2, rows, width, size), BF16),
            pltpu.VMEM((2, rows, width, block), BF16),
            pltpu.VMEM((2, rows, width, block), BF16),
            pltpu.VMEM((2, rows, width, block), BF16),
            pltpu.VMEM((width, piece), F32),
            pltpu.VMEM((strip, piece), F32),
            pltpu.VMEM((layer, width, piece), F32),
            pltpu.VMEM((layer, strip, piece), F32),
            pltpu.VMEM((layer, width, piece), BF16),
            pltpu.VMEM((layer, strip, piece), BF16),
            pltpu.VMEM((layer - 1, width, piece), BF16),
            pltpu.VMEM((layer - 1, strip, piece), BF16),
            pltpu.VMEM((strip, piece), BF16),
            pltpu.VMEM((rows - 1, strip, piece), BF16),
            dma((rows - 1, poles - 1)),
            dma((rows - 1, poles - 1)),
            dma((10,)),
            dma((rows - 1,)),
            dma((rows - 1,)),
            dma((rows - 1,)),
            dma((rows - 1,)),
            dma((layer - 1,)),
            dma((layer - 1,)),
            dma((layer - 1,)),
            dma((layer - 1,)),
            dma((rows - 1,)),
            dma((rows - 1,)),
            dma((cols - 1,)),
            dma((cols - 1,)),
            dma((3,)),
        ],
        compiler_params=pltpu.CompilerParams(
            collective_id=0, has_side_effects=True, vmem_limit_bytes=60 * 1024 * 1024
        ),
        name="front_step",
    )(
        pole_shift,
        pole_weight,
        pattern,
        front_h,
        front_s,
        panel_h,
        panel_s,
        pivot_h,
        pivot_s,
        ancestor,
    )
    schur, rows_out, pivot_out = pl.pallas_call(
        hand_over,
        out_shape=out_shape,
        in_specs=[hbm] * 3,
        out_specs=(hbm,) * 3,
        scratch_shapes=[pltpu.VMEM(part.shape, part.dtype) for part in out_shape]
        + [dma((2, 3))],
        compiler_params=pltpu.CompilerParams(vmem_limit_bytes=60 * 1024 * 1024),
        name="hand_over",
    )(*found)
    return (
        schur.reshape(ancestor_inverse.shape),
        rows_out,
        pivot_out.reshape(size, piece),
    )


def solution(mesh):
    sizes = dict(mesh.shape)
    in_specs = (
        P(("row", "col"), None),
        P(("row", "col"), None),
        P("row", None),
        P("row", None),
        P(),
        P(),
        P("pole", None),
        P("pole", None),
        P(),
        P("pole", None, None, "col", None, "row"),
    )
    out_specs = (
        P("pole", None, None, "col", None, "row"),
        P(("row", "col"), "pole"),
        P(None, "pole"),
    )
    body = functools.partial(shards, sizes["row"], sizes["col"], sizes["pole"])
    return jax.shard_map(body, mesh=mesh, in_specs=in_specs, out_specs=out_specs, check_vma=False)
```
